128 devices in a mesh: site: 2 (over core), blk: 64 (over y, x, z).
Axes of the slice: x: 4, y: 4, z: 4, core: 2. Of those that a mesh axis runs over, the one named last changes fastest.
Arguments:
- env_in: float32 [3, 128, 512, 512], P(None, 'blk'), may hold values from -6 to 6
- site_tensor: float32 [2, 128, 3, 512, 512], P('site', 'blk'), may hold values from -0.25 to 0.25
- pair_live: int32 [2, 128, 3], P('site', 'blk'), may hold values 0 or 1
- coef_index: int32 [2, 128, 3], P('site', 'blk'), may hold values from 0 to 3
- mpo_coef: float32 [2, 4], P('site'), may hold values from 0.5 to 1.5
Outputs:
- env_out: float32 [2, 3, 128, 512, 512], P('site', None, 'blk')
The draws below stay inside these ranges and needn't reach their ends.
All inputs are finite; a program needn't handle non-finite values. No bound on the sum of `pair_live` on one device may be relied on, other than what follows from the above.
Results may differ from the reference program's by a relative error of at most 0.00014.
Values sent between devices are 32-bit elements; how exact they have to be, the bound alone decides.
No kernel may reach another device: no remote copies, remote signals or barrier semaphores. Data moves between devices by JAX's collectives and lax.ppermute only.
A program may use at most 128 MiB of HBM per device.

```python
import jax
import jax.numpy as jnp
from jax import lax

BW = 512
STATES = 3
SLOTS = 3
NCOEF = 4
SITES = 2
SECTORS = 128


def place_ends(entries, stream_key, smallest, top_value):
    place = [jax.random.randint(jax.random.fold_in(stream_key, axis), (), 0, length) for axis, length in enumerate(entries.shape)]
    longest = entries.shape.index(max(entries.shape))
    neighbour = place[:longest] + [(place[longest] + 1) % entries.shape[longest]] + place[longest + 1:]
    return entries.at[tuple(place)].set(smallest).at[tuple(neighbour)].set(top_value)


def steps_of(rng, extent, split, smallest, high):
    level, own = 1.0, jax.random.fold_in(rng, 6)
    for dim, parts in split:
        steps = jnp.exp(jax.random.uniform(jax.random.fold_in(own, dim), (parts,), jnp.float32, smallest / len(split), high / len(split)))
        level = level * jnp.repeat(steps, extent[dim] // parts).reshape([-1 if axis == dim else 1 for axis in range(len(extent))])
    return level


def noise(key, extent, spread, reach, cuts=(), kind=jnp.bfloat16):
    factor_of = steps_of(key, extent, cuts, -0.22, 0.18) if cuts else 1.0
    entries = jax.random.normal(key, extent, jnp.float32) * spread * factor_of
    return jnp.minimum(jnp.maximum(entries, -reach), reach).astype(kind)


def setup_inputs(seed: int = 0) -> dict:
    arg_keys = jax.random.split(jax.random.key(seed), 6)
    return {
        "env_in": noise(arg_keys[0], (STATES, SECTORS, BW, BW), 1.0, 6.0, ((1, 64),), jnp.float32),
        "site_tensor": noise(arg_keys[1], (SITES, SECTORS, SLOTS, BW, BW), BW ** -0.5, 0.25, ((0, 2), (1, 64)), jnp.float32),
        "pair_live": place_ends((jax.random.randint(arg_keys[2], (SITES, SECTORS, SLOTS), 0, 3) < 2).astype(jnp.int32), jax.random.fold_in(arg_keys[2], 1), 0, 1),
        "coef_index": place_ends(jax.random.randint(arg_keys[3], (SITES, SECTORS, SLOTS), 0, NCOEF), jax.random.fold_in(arg_keys[3], 1), 0, NCOEF - 1).astype(jnp.int32),
        "mpo_coef": jnp.clip(0.5 + 1.0 * jax.random.uniform(arg_keys[4], (SITES, NCOEF), jnp.float32) ** steps_of(arg_keys[4], (SITES, NCOEF), ((0, 2),), -0.2, 0.2), 0.5, 1.5),
    }


def reference(env_in, site_tensor, pair_live, coef_index, mpo_coef):
    environ = env_in
    stacked = []
    for site_no in range(SITES):
        zeros_rim = jnp.zeros((STATES, 1, BW, BW), jnp.float32)
        padded = jnp.concatenate([zeros_rim, environ, zeros_rim], 1)
        weights_all = pair_live[site_no].astype(jnp.float32) * mpo_coef[site_no][coef_index[site_no]]

        def per_sector(mapped):
            tensors, weights, sector = mapped
            summed = jnp.zeros((STATES, BW, BW), jnp.float32)
            for slot_index in range(SLOTS):
                source = lax.dynamic_index_in_dim(padded, sector + slot_index, 1, keepdims=False)
                half_product = jnp.einsum("xi,nxy->niy", tensors[slot_index], source, precision=lax.Precision.HIGHEST)
                summed = summed + weights[slot_index] * jnp.einsum("niy,yc->nic", half_product, tensors[slot_index], precision=lax.Precision.HIGHEST)
            return summed

        updated = lax.map(per_sector, (site_tensor[site_no], weights_all, jnp.arange(SECTORS, dtype=jnp.int32)))
        environ = jnp.transpose(updated, (1, 0, 2, 3))
        stacked.append(environ)
    return jnp.stack(stacked)
```

```python
import functools

import jax
import jax.numpy as jnp
from jax import lax
from jax.experimental import pallas as pl
from jax.experimental.pallas import tpu as pltpu
from jax.sharding import PartitionSpec as P

F32 = jnp.float32
BF16 = jnp.bfloat16
LIMIT = 28 << 20

STORE = 6
CUTS = 2


def split(x):
    high = x.astype(BF16)
    return high, (x - high.astype(F32)).astype(BF16)


def dot_nn(a, b):
    return jnp.dot(a, b, preferred_element_type=F32)


def dot_nt(a, b):
    return lax.dot_general(a, b, (((1,), (1,)), ((), ())), preferred_element_type=F32)


def sandwich(block, high, low):
    block_high, block_low = split(block)
    inner = dot_nt(block_high, high) + dot_nt(block_high, low) + dot_nt(block_low, high)
    inner_high, inner_low = split(inner)
    return dot_nn(high, inner_high) + dot_nn(low, inner_high) + dot_nn(high, inner_low)


def cost():
    return pl.CostEstimate(flops=0, bytes_accessed=1024, transcendentals=0)


def params():
    return pltpu.CompilerParams(vmem_limit_bytes=LIMIT)


def root(live_ref, index_ref, coef_ref, sector, slot, width):
    weight = live_ref[0, sector, slot].astype(F32) * coef_ref[0, index_ref[0, sector, slot]]
    return jnp.sqrt(jnp.full((1, width), weight, F32))


def slot_at(k, c):
    return jnp.where(k == 0, 1, jnp.where(k == 1, 2 - 2 * c, 2 * c))


SCALARS = [pl.BlockSpec(memory_space=pltpu.SMEM)] * 3
HBM_REF = pl.BlockSpec(memory_space=pl.ANY)


def edge(core, env, first, count):
    width = env.shape[-1]
    parts = 4
    rows = width // parts

    def kernel(core_ref, e_ref, o_ref, sems):
        copies = []
        for n in range(count):
            for p in range(parts):
                span = pl.ds(p * rows, rows)
                copies.append(pltpu.make_async_copy(e_ref.at[first + n, core_ref[0], span], o_ref.at[n, span], sems.at[n * parts + p]))
        for copy in copies:
            copy.start()
        for copy in copies:
            copy.wait()

    return pl.pallas_call(
        kernel,
        grid_spec=pltpu.PrefetchScalarGridSpec(
            num_scalar_prefetch=1,
            grid=(1,),
            in_specs=[HBM_REF],
            out_specs=pl.BlockSpec(memory_space=pltpu.VMEM),
            scratch_shapes=[pltpu.SemaphoreType.DMA((count * parts,))],
        ),
        out_shape=jax.ShapeDtypeStruct((count, width, width), F32),
        compiler_params=params(),
        cost_estimate=cost(),
        name=f"edge_{first}",
    )(core, env)


def outgoing(core, scalars, tensors, after):
    width = tensors.shape[-1]

    def kernel(core_ref, live_ref, index_ref, coef_ref, t_ref, after_ref, *o_refs):
        other = 1 - core_ref[0]
        for k, o_ref in enumerate(o_refs):
            slot = slot_at(k, other)
            o_ref[...] = t_ref[0, 0, slot] * root(live_ref, index_ref, coef_ref, other, slot, width)

    return pl.pallas_call(
        kernel,
        grid_spec=pltpu.PrefetchScalarGridSpec(
            num_scalar_prefetch=1,
            grid=(1,),
            in_specs=SCALARS + [pl.BlockSpec((1, 1, 3, width, width), lambda k, c: (0, 1 - c[0], 0, 0, 0)), HBM_REF],
            out_specs=[pl.BlockSpec((width, width), lambda k, c: (0, 0))] * 3,
        ),
        out_shape=[jax.ShapeDtypeStruct((width, width), F32)] * 3,
        compiler_params=params(),
        cost_estimate=cost(),
        name="outgoing",
    )(core, *scalars, tensors, after)


def own_store(core, scalars, tensors, after):
    width = tensors.shape[-1]

    def kernel(core_ref, live_ref, index_ref, coef_ref, t_ref, after_ref, o_ref):
        c = core_ref[0]
        slot = slot_at(pl.program_id(0), c)
        high, low = split((t_ref[0, 0, 0] * root(live_ref, index_ref, coef_ref, c, slot, width)).T)
        o_ref[0, 0] = high
        o_ref[0, 1] = low

    return pl.pallas_call(
        kernel,
        grid_spec=pltpu.PrefetchScalarGridSpec(
            num_scalar_prefetch=1,
            grid=(3,),
            in_specs=SCALARS + [pl.BlockSpec((1, 1, 1, width, width), lambda k, c: (0, c[0], slot_at(k, c[0]), 0, 0)), HBM_REF],
            out_specs=pl.BlockSpec((1, 2, width, width), lambda k, c: (k, 0, 0, 0)),
        ),
        out_shape=jax.ShapeDtypeStruct((STORE, 2, width, width), BF16),
        compiler_params=params(),
        cost_estimate=cost(),
        name="own_store",
    )(core, *scalars, tensors, after)


def full_store(store, received):
    width = store.shape[-1]

    def kernel(*refs):
        o_ref = refs[-1]
        for k in range(3):

            @pl.when(pl.program_id(0) == k)
            def _():
                high, low = split(refs[k][...].T)
                o_ref[0, 0] = high
                o_ref[0, 1] = low

    return pl.pallas_call(
        kernel,
        grid=(3,),
        in_specs=[pl.BlockSpec((width, width), lambda k: (0, 0))] * 3 + [HBM_REF],
        out_specs=pl.BlockSpec((1, 2, width, width), lambda k: (k + 3, 0, 0, 0)),
        out_shape=jax.ShapeDtypeStruct(store.shape, BF16),
        input_output_aliases={3: 0},
        compiler_params=params(),
        cost_estimate=cost(),
        name="full_store",
    )(*received, store)


def near_terms(core, site, own, other, in_env, store, after):
    states, width = own.shape[0], own.shape[-1]

    def kernel(core_ref, a_ref, b_ref, ta_ref, tb_ref, *refs):
        o_ref = refs[-1]
        a, b = (a_ref[0, 0], b_ref[0, 0]) if in_env else (a_ref[0], b_ref[0])
        o_ref[0] = sandwich(a, ta_ref[0, 0], ta_ref[0, 1]) + sandwich(b, tb_ref[0, 0], tb_ref[0, 1])

    def slot(k):
        return lambda n, c: ((3 * c[0] if site == 0 else 3 - 3 * c[0]) + k, 0, 0, 0)

    row = pl.BlockSpec((1, width, width), lambda n, c: (n, 0, 0))
    sources = [row, row]
    if in_env:
        block = (1, 1, width, width)
        sources = [pl.BlockSpec(block, lambda n, c: (n, c[0], 0, 0)), pl.BlockSpec(block, lambda n, c: (n, 1 - c[0], 0, 0))]
    pair = (1, 2, width, width)
    return pl.pallas_call(
        kernel,
        grid_spec=pltpu.PrefetchScalarGridSpec(
            num_scalar_prefetch=1,
            grid=(states,),
            in_specs=sources + [pl.BlockSpec(pair, slot(0)), pl.BlockSpec(pair, slot(1))] + [HBM_REF] * len(after),
            out_specs=row,
        ),
        out_shape=jax.ShapeDtypeStruct((states, width, width), F32),
        compiler_params=params(),
        cost_estimate=cost(),
        name=f"near_terms_{site}",
    )(core, own, other, store, store, *after)


def far_term(core, site, partial, row, halo, halo_row, store, after):
    width = halo.shape[-1]

    def kernel(core_ref, p_ref, h_ref, t_ref, *refs):
        refs[-1][...] = p_ref[...] + sandwich(h_ref[0], t_ref[0, 0], t_ref[0, 1])[None]

    return pl.pallas_call(
        kernel,
        grid_spec=pltpu.PrefetchScalarGridSpec(
            num_scalar_prefetch=1,
            grid=(1,),
            in_specs=[
                pl.BlockSpec((1, width, width), lambda n, c: (row, 0, 0)),
                pl.BlockSpec((1, width, width), lambda n, c: (halo_row, 0, 0)),
                pl.BlockSpec((1, 2, width, width), lambda n, c: ((3 * c[0] if site == 0 else 3 - 3 * c[0]) + 2, 0, 0, 0)),
            ]
            + [HBM_REF] * len(after),
            out_specs=pl.BlockSpec((1, width, width), lambda n, c: (0, 0, 0)),
        ),
        out_shape=jax.ShapeDtypeStruct((1, width, width), F32),
        compiler_params=params(),
        cost_estimate=cost(),
        name=f"far_term_{site}",
    )(core, partial, halo, store, *after)


def write_rows(core, out, shape, moves, sources, name):
    width = shape[-1]
    count = len(sources)

    def kernel(core_ref, *refs):
        o_ref, sems = refs[count + len(old)], refs[-1]
        if not old:
            refs[count + 1][...] = jnp.zeros((8, 128), F32)
        for c in range(2):

            @pl.when(core_ref[0] == c)
            def _():
                copies = [
                    pltpu.make_async_copy(refs[i].at[0], o_ref.at[state, sector], sems.at[m])
                    for m, (i, state, sector) in enumerate(moves[c])
                ]
                for copy in copies:
                    copy.start()
                for copy in copies:
                    copy.wait()

    old = [] if out is None else [out]
    outs = [jax.ShapeDtypeStruct(shape, F32)]
    if not old:
        outs.append(jax.ShapeDtypeStruct((8, 128), F32))
    return pl.pallas_call(
        kernel,
        grid_spec=pltpu.PrefetchScalarGridSpec(
            num_scalar_prefetch=1,
            grid=(1,),
            in_specs=[pl.BlockSpec(memory_space=pltpu.VMEM)] * count + [HBM_REF] * len(old),
            out_specs=[HBM_REF, pl.BlockSpec(memory_space=pltpu.VMEM)][: len(outs)],
            scratch_shapes=[pltpu.SemaphoreType.DMA((6,))],
        ),
        out_shape=outs,
        input_output_aliases={count + 1: 0} if old else {},
        compiler_params=params(),
        cost_estimate=cost(),
        name=name,
    )(core, *sources, *old)


def shards(chips, env_in, site_tensor, pair_live, coef_index, mpo_coef):
    axes = ("site", "blk")
    core = jnp.reshape(lax.axis_index("site"), (1,)).astype(jnp.int32)
    swap = [(s * chips + j, (1 - s) * chips + j) for s in range(2) for j in range(chips)]
    meet = [(chips + j, j + 1) for j in range(chips - 1)] + [(j + 1, chips + j) for j in range(chips - 1)]
    down = [(j, chips + j) for j in range(chips)]

    def send(value, pairs):
        return lax.ppermute(value, axes, pairs)

    scalars = (pair_live, coef_index, mpo_coef)
    pinned = pltpu.with_memory_space_constraint(env_in, pltpu.HBM)
    edge_a = edge(core, pinned, 0, CUTS)
    halo_a = send(edge_a, meet)
    leaving = outgoing(core, scalars, site_tensor, edge_a)
    received = [send(block, swap) for block in leaving]
    store = own_store(core, scalars, site_tensor, leaving[0])
    edge_b = edge(core, pinned, CUTS, 3 - CUTS)
    halo_b = send(edge_b, meet)
    store = full_store(store, received)

    near = near_terms(core, 0, env_in, env_in, True, store, [])
    first, crossed, halos = [], [], []
    for n in range(3):
        halo, row = (halo_a, n) if n < CUTS else (halo_b, n - CUTS)
        first.append(far_term(core, 0, near, n, halo, row, store, first[-1:]))
        halos.append(send(first[n], meet))
        crossed.append(send(first[n], swap))

    second, moved, token, sums = [], [], [], []
    for n in range(3):
        if n == 2:
            early = [(0, 0, 0), (1, 0, 1), (2, 1, 0), (3, 1, 1)], [(4, 0, 1), (5, 1, 1)]
            out, mark = write_rows(core, None, env_in.shape, early, [first[0], crossed[0], first[1], crossed[1], second[0], second[1]], "early_rows")
            token = [mark]
        sums.append(near_terms(core, 1, first[n], crossed[n], False, store, sums[-1:]))
        second.append(far_term(core, 1, sums[n], 0, halos[n], 0, store, token))
        moved.append(send(second[n], down))
    late = [(0, 2, 0), (1, 2, 1)], [(2, 0, 0), (3, 1, 0), (4, 2, 0), (5, 2, 1)]
    (out,) = write_rows(core, out, env_in.shape, late, [first[2], crossed[2], *moved, second[2]], "late_rows")
    return out[None]


def solution(mesh):
    return jax.shard_map(
        functools.partial(shards, mesh.shape["blk"]),
        mesh=mesh,
        in_specs=(
            P(None, "blk", None, None),
            P("site", "blk", None, None, None),
            P("site", "blk", None),
            P("site", "blk", None),
            P("site", None),
        ),
        out_specs=P("site", None, "blk", None, None),
        check_vma=False,
    )
```

```python
import functools

import jax
import jax.numpy as jnp
from jax import lax
from jax.experimental import pallas as pl
from jax.experimental.pallas import tpu as pltpu
from jax.sharding import PartitionSpec as P

F32 = jnp.float32
BF16 = jnp.bfloat16
LIMIT = 28 << 20

STORE = 6
CUTS = 2
PARTS = 2


def split(x):
    high = x.astype(BF16)
    return high, (x - high.astype(F32)).astype(BF16)


def dot_nn(a, b):
    return jnp.dot(a, b, preferred_element_type=F32)


def dot_nt(a, b):
    return lax.dot_general(a, b, (((1,), (1,)), ((), ())), preferred_element_type=F32)


def sandwich(block, high, low):
    block_high, block_low = split(block)
    inner = dot_nt(block_high, high) + dot_nt(block_high, low) + dot_nt(block_low, high)
    inner_high, inner_low = split(inner)
    return dot_nn(high, inner_high) + dot_nn(low, inner_high) + dot_nn(high, inner_low)


def cost(weight=0.0):
    return pl.CostEstimate(flops=int(weight * 1.15e9), bytes_accessed=1024, transcendentals=0)


def params():
    return pltpu.CompilerParams(vmem_limit_bytes=LIMIT)


def root(live_ref, index_ref, coef_ref, sector, slot, width):
    weight = live_ref[0, sector, slot].astype(F32) * coef_ref[0, index_ref[0, sector, slot]]
    return jnp.sqrt(jnp.full((1, width), weight, F32))


def slot_at(k, c):
    return jnp.where(k == 0, 1, jnp.where(k == 1, 2 - 2 * c, 2 * c))


SCALARS = [pl.BlockSpec(memory_space=pltpu.SMEM)] * 3
HBM_REF = pl.BlockSpec(memory_space=pl.ANY)


def edge(core, env):
    width = env.shape[-1]
    parts = 4
    rows = width // parts

    def kernel(core_ref, e_ref, o_ref, sems):
        copies = []
        for n in range(CUTS):
            for p in range(parts):
                span = pl.ds(p * rows, rows)
                copies.append(pltpu.make_async_copy(e_ref.at[n, core_ref[0], span], o_ref.at[n, span], sems.at[n * parts + p]))
        for copy in copies:
            copy.start()
        for copy in copies:
            copy.wait()

    return pl.pallas_call(
        kernel,
        grid_spec=pltpu.PrefetchScalarGridSpec(
            num_scalar_prefetch=1,
            grid=(1,),
            in_specs=[HBM_REF],
            out_specs=pl.BlockSpec(memory_space=pltpu.VMEM),
            scratch_shapes=[pltpu.SemaphoreType.DMA((CUTS * parts,))],
        ),
        out_shape=jax.ShapeDtypeStruct((CUTS, width, width), F32),
        compiler_params=params(),
        cost_estimate=cost(),
        name="edge",
    )(core, env)


def outgoing(core, scalars, tensors, after):
    width = tensors.shape[-1]

    def kernel(core_ref, live_ref, index_ref, coef_ref, t_ref, after_ref, *o_refs):
        other = 1 - core_ref[0]
        for k, o_ref in enumerate(o_refs):
            slot = slot_at(k, other)
            o_ref[...] = t_ref[0, 0, slot] * root(live_ref, index_ref, coef_ref, other, slot, width)

    return pl.pallas_call(
        kernel,
        grid_spec=pltpu.PrefetchScalarGridSpec(
            num_scalar_prefetch=1,
            grid=(1,),
            in_specs=SCALARS + [pl.BlockSpec((1, 1, 3, width, width), lambda k, c: (0, 1 - c[0], 0, 0, 0)), HBM_REF],
            out_specs=[pl.BlockSpec((width, width), lambda k, c: (0, 0))] * 3,
        ),
        out_shape=[jax.ShapeDtypeStruct((width, width), F32)] * 3,
        compiler_params=params(),
        cost_estimate=cost(),
        name="outgoing",
    )(core, *scalars, tensors, after)


def own_store(core, scalars, tensors, env, after):
    width = tensors.shape[-1]

    def kernel(core_ref, live_ref, index_ref, coef_ref, t_ref, e_ref, after_ref, o_ref, edge_ref, sems):
        c = core_ref[0]
        slot = slot_at(pl.program_id(0), c)
        parts = 4
        copies = []
        for p in range(parts):
            span = pl.ds(p * (width // parts), width // parts)
            for n in range(3 - CUTS):
                copies.append(pltpu.make_async_copy(e_ref.at[CUTS + n, c, span], edge_ref.at[n, span], sems.at[n * parts + p]))

        @pl.when(pl.program_id(0) == 0)
        def _():
            for copy in copies:
                copy.start()

        high, low = split((t_ref[0, 0, 0] * root(live_ref, index_ref, coef_ref, c, slot, width)).T)
        o_ref[0, 0] = high
        o_ref[0, 1] = low

        @pl.when(pl.program_id(0) == 2)
        def _():
            for copy in copies:
                copy.wait()

    return pl.pallas_call(
        kernel,
        grid_spec=pltpu.PrefetchScalarGridSpec(
            num_scalar_prefetch=1,
            grid=(3,),
            in_specs=SCALARS + [pl.BlockSpec((1, 1, 1, width, width), lambda k, c: (0, c[0], slot_at(k, c[0]), 0, 0)), HBM_REF, HBM_REF],
            out_specs=[pl.BlockSpec((1, 2, width, width), lambda k, c: (k, 0, 0, 0)), pl.BlockSpec(memory_space=pltpu.VMEM)],
            scratch_shapes=[pltpu.SemaphoreType.DMA((4 * (3 - CUTS),))],
        ),
        out_shape=[jax.ShapeDtypeStruct((STORE, 2, width, width), BF16), jax.ShapeDtypeStruct((3 - CUTS, width, width), F32)],
        compiler_params=params(),
        cost_estimate=cost(),
        name="own_store",
    )(core, *scalars, tensors, env, after)


def full_store(store, received):
    width = store.shape[-1]

    def kernel(*refs):
        o_ref = refs[-1]
        for k in range(3):

            @pl.when(pl.program_id(0) == k)
            def _():
                high, low = split(refs[k][...].T)
                o_ref[0, 0] = high
                o_ref[0, 1] = low

    return pl.pallas_call(
        kernel,
        grid=(3,),
        in_specs=[pl.BlockSpec((width, width), lambda k: (0, 0))] * 3 + [HBM_REF],
        out_specs=pl.BlockSpec((1, 2, width, width), lambda k: (k + 3, 0, 0, 0)),
        out_shape=jax.ShapeDtypeStruct(store.shape, BF16),
        input_output_aliases={3: 0},
        compiler_params=params(),
        cost_estimate=cost(),
        name="full_store",
    )(*received, store)


def near_terms(core, site, own, other, in_env, store, after):
    states, width = own.shape[0], own.shape[-1]

    def kernel(core_ref, a_ref, b_ref, ta_ref, tb_ref, *refs):
        o_ref = refs[-1]
        a, b = (a_ref[0, 0], b_ref[0, 0]) if in_env else (a_ref[0], b_ref[0])
        o_ref[0] = sandwich(a, ta_ref[0, 0], ta_ref[0, 1]) + sandwich(b, tb_ref[0, 0], tb_ref[0, 1])

    def slot(k):
        return lambda n, c: ((3 * c[0] if site == 0 else 3 - 3 * c[0]) + k, 0, 0, 0)

    row = pl.BlockSpec((1, width, width), lambda n, c: (n, 0, 0))
    sources = [row, row]
    if in_env:
        block = (1, 1, width, width)
        sources = [pl.BlockSpec(block, lambda n, c: (n, c[0], 0, 0)), pl.BlockSpec(block, lambda n, c: (n, 1 - c[0], 0, 0))]
    pair = (1, 2, width, width)
    return pl.pallas_call(
        kernel,
        grid_spec=pltpu.PrefetchScalarGridSpec(
            num_scalar_prefetch=1,
            grid=(states,),
            in_specs=sources + [pl.BlockSpec(pair, slot(0)), pl.BlockSpec(pair, slot(1))] + [HBM_REF] * len(after),
            out_specs=row,
        ),
        out_shape=jax.ShapeDtypeStruct((states, width, width), F32),
        compiler_params=params(),
        cost_estimate=cost(),
        name=f"near_terms_{site}",
    )(core, own, other, store, store, *after)


def far_terms(core, site, partial, first, halo, store, parts, weight, after):
    states, width = halo.shape[0], halo.shape[-1]
    rows = width // parts

    def kernel(core_ref, p_ref, h_ref, t_ref, *refs):
        total = p_ref[0] + sandwich(h_ref[0], t_ref[0, 0], t_ref[0, 1])
        for p in range(parts):
            refs[len(after) + p][0] = total[p * rows : (p + 1) * rows]

    return pl.pallas_call(
        kernel,
        grid_spec=pltpu.PrefetchScalarGridSpec(
            num_scalar_prefetch=1,
            grid=(states,),
            in_specs=[
                pl.BlockSpec((1, width, width), lambda n, c: (n + first, 0, 0)),
                pl.BlockSpec((1, width, width), lambda n, c: (n, 0, 0)),
                pl.BlockSpec((1, 2, width, width), lambda n, c: ((3 * c[0] if site == 0 else 3 - 3 * c[0]) + 2, 0, 0, 0)),
            ]
            + [HBM_REF] * len(after),
            out_specs=[pl.BlockSpec((1, rows, width), lambda n, c: (n, 0, 0))] * parts,
        ),
        out_shape=[jax.ShapeDtypeStruct((states, rows, width), F32)] * parts,
        compiler_params=params(),
        cost_estimate=cost(weight),
        name=f"far_terms_{site}",
    )(core, partial, halo, store, *after)


def write_rows(core, out, shape, moves, name):
    width = shape[-1]
    sources = [block for c in range(2) for blocks, _, _ in moves[c] for block in blocks]
    count = len(sources)
    old = [] if out is None else [out]

    def kernel(core_ref, *refs):
        o_ref, sems = refs[count + len(old)], refs[-1]
        if not old:
            refs[count + 1][...] = jnp.zeros((8, 128), F32)
        at = 0
        plans = []
        for c in range(2):
            plan = []
            for blocks, state, sector in moves[c]:
                rows = width // len(blocks)
                for p in range(len(blocks)):
                    plan += [(at, n, state + n, sector, p * rows, rows) for n in range(blocks[p].shape[0])]
                    at += 1
            plans.append(plan)
        for c in range(2):

            @pl.when(core_ref[0] == c)
            def _():
                copies = [
                    pltpu.make_async_copy(refs[i].at[n], o_ref.at[state, sector, pl.ds(begin, rows)], sems.at[m])
                    for m, (i, n, state, sector, begin, rows) in enumerate(plans[c])
                ]
                for copy in copies:
                    copy.start()
                for copy in copies:
                    copy.wait()

    outs = [jax.ShapeDtypeStruct(shape, F32)]
    if not old:
        outs.append(jax.ShapeDtypeStruct((8, 128), F32))
    return pl.pallas_call(
        kernel,
        grid_spec=pltpu.PrefetchScalarGridSpec(
            num_scalar_prefetch=1,
            grid=(1,),
            in_specs=[pl.BlockSpec(memory_space=pltpu.VMEM)] * count + [HBM_REF] * len(old),
            out_specs=[HBM_REF, pl.BlockSpec(memory_space=pltpu.VMEM)][: len(outs)],
            scratch_shapes=[pltpu.SemaphoreType.DMA((16,))],
        ),
        out_shape=outs,
        input_output_aliases={count + 1: 0} if old else {},
        compiler_params=params(),
        cost_estimate=cost(),
        name=name,
    )(core, *sources, *old)


def shards(chips, env_in, site_tensor, pair_live, coef_index, mpo_coef):
    axes = ("site", "blk")
    core = jnp.reshape(lax.axis_index("site"), (1,)).astype(jnp.int32)
    swap = [(s * chips + j, (1 - s) * chips + j) for s in range(2) for j in range(chips)]
    meet = [(chips + j, j + 1) for j in range(chips - 1)] + [(j + 1, chips + j) for j in range(chips - 1)]

    def send(value, pairs):
        return lax.ppermute(value, axes, pairs)

    scalars = (pair_live, coef_index, mpo_coef)
    pinned = pltpu.with_memory_space_constraint(env_in, pltpu.HBM)
    edge_a = edge(core, pinned)
    halo_a = send(edge_a, meet)
    leaving = outgoing(core, scalars, site_tensor, edge_a)
    received = [send(block, swap) for block in leaving]
    store, edge_b = own_store(core, scalars, site_tensor, pinned, leaving[0])
    halo_b = send(edge_b, meet)
    store = full_store(store, received)

    near = near_terms(core, 0, env_in, env_in, True, store, [])
    first_a, = far_terms(core, 0, near, 0, halo_a, store, 1, 0, [])
    second_halo_a, crossed_a = send(first_a, meet), send(first_a, swap)
    first_b, = far_terms(core, 0, near, CUTS, halo_b, store, 1, 16, [first_a])
    second_halo_b, crossed_b = send(first_b, meet), send(first_b, swap)

    near_a = near_terms(core, 1, first_a, crossed_a, False, store, [])
    near_b = near_terms(core, 1, first_b, crossed_b, False, store, [near_a])
    second_a = far_terms(core, 1, near_a, 0, second_halo_a, store, 2 * PARTS, 0, [near_b])
    moved_a = [send(block, swap) for block in second_a]
    early = [([first_a], 0, 0), ([crossed_a], 0, 1)], [(moved_a, 0, 0), (second_a, 0, 1)]
    out, mark = write_rows(core, None, env_in.shape, early, "early_rows")
    second_b = far_terms(core, 1, near_b, 0, second_halo_b, store, PARTS, 0, [mark])
    moved_b = [send(block, swap) for block in second_b]
    middle = [([first_b], CUTS, 0), ([crossed_b], CUTS, 1)], [(second_b, CUTS, 1)]
    (out,) = write_rows(core, out, env_in.shape, middle, "middle_rows")
    (out,) = write_rows(core, out, env_in.shape, ([], [(moved_b, CUTS, 0)]), "late_rows")
    return out[None]


def solution(mesh):
    return jax.shard_map(
        functools.partial(shards, mesh.shape["blk"]),
        mesh=mesh,
        in_specs=(
            P(None, "blk", None, None),
            P("site", "blk", None, None, None),
            P("site", "blk", None),
            P("site", "blk", None),
            P("site", None),
        ),
        out_specs=P("site", None, "blk", None, None),
        check_vma=False,
    )
```

```python
import functools

import jax
import jax.numpy as jnp
from jax import lax
from jax.experimental import pallas as pl
from jax.experimental.pallas import tpu as pltpu
from jax.sharding import PartitionSpec as P

F32 = jnp.float32
BF16 = jnp.bfloat16
LIMIT = 28 << 20

STORE = 7
CUTS = 2
PARTS = 1
HALVES = 2


def split(x):
    high = x.astype(BF16)
    return high, (x - high.astype(F32)).astype(BF16)


def dot_nn(a, b):
    return jnp.dot(a, b, preferred_element_type=F32)


def dot_nt(a, b):
    return lax.dot_general(a, b, (((1,), (1,)), ((), ())), preferred_element_type=F32)


def inner_halves(block, high, low):
    block_high, block_low = split(block)
    return split(dot_nt(block_high, high) + dot_nt(block_high, low) + dot_nt(block_low, high))


def outer(high, low, inner_high, inner_low):
    return dot_nn(high, inner_high) + dot_nn(low, inner_high) + dot_nn(high, inner_low)


def sandwich(block, high, low):
    return outer(high, low, *inner_halves(block, high, low))


def cost(weight=0.0):
    return pl.CostEstimate(flops=int(weight * 1.15e9), bytes_accessed=1024, transcendentals=0)


def params():
    return pltpu.CompilerParams(vmem_limit_bytes=LIMIT)


def root(live_ref, index_ref, coef_ref, sector, slot, width):
    weight = live_ref[0, sector, slot].astype(F32) * coef_ref[0, index_ref[0, sector, slot]]
    return jnp.sqrt(jnp.full((1, width), weight, F32))


def slot_at(k, c):
    return jnp.where(k == 0, 1, jnp.where(k == 1, 2 - 2 * c, 2 * c))


SCALARS = [pl.BlockSpec(memory_space=pltpu.SMEM)] * 3
HBM_REF = pl.BlockSpec(memory_space=pl.ANY)


def edge(core, env):
    width = env.shape[-1]
    parts = 4
    rows = width // parts

    def kernel(core_ref, e_ref, o_ref, sems):
        copies = []
        for n in range(CUTS):
            for p in range(parts):
                span = pl.ds(p * rows, rows)
                copies.append(pltpu.make_async_copy(e_ref.at[n, core_ref[0], span], o_ref.at[n, span], sems.at[n * parts + p]))
        for copy in copies:
            copy.start()
        for copy in copies:
            copy.wait()

    return pl.pallas_call(
        kernel,
        grid_spec=pltpu.PrefetchScalarGridSpec(
            num_scalar_prefetch=1,
            grid=(1,),
            in_specs=[HBM_REF],
            out_specs=pl.BlockSpec(memory_space=pltpu.VMEM),
            scratch_shapes=[pltpu.SemaphoreType.DMA((CUTS * parts,))],
        ),
        out_shape=jax.ShapeDtypeStruct((CUTS, width, width), F32),
        compiler_params=params(),
        cost_estimate=cost(),
        name="edge",
    )(core, env)


def outgoing(core, scalars, tensors, after):
    width = tensors.shape[-1]

    def kernel(core_ref, live_ref, index_ref, coef_ref, t_ref, after_ref, *o_refs):
        other = 1 - core_ref[0]
        for k, o_ref in enumerate(o_refs):
            slot = slot_at(k, other)
            o_ref[...] = t_ref[0, 0, slot] * root(live_ref, index_ref, coef_ref, other, slot, width)

    return pl.pallas_call(
        kernel,
        grid_spec=pltpu.PrefetchScalarGridSpec(
            num_scalar_prefetch=1,
            grid=(1,),
            in_specs=SCALARS + [pl.BlockSpec((1, 1, 3, width, width), lambda k, c: (0, 1 - c[0], 0, 0, 0)), HBM_REF],
            out_specs=[pl.BlockSpec((width, width), lambda k, c: (0, 0))] * 3,
        ),
        out_shape=[jax.ShapeDtypeStruct((width, width), F32)] * 3,
        compiler_params=params(),
        cost_estimate=cost(),
        name="outgoing",
    )(core, *scalars, tensors, after)


def own_store(core, scalars, tensors, env, after):
    width = tensors.shape[-1]

    def kernel(core_ref, live_ref, index_ref, coef_ref, t_ref, e_ref, after_ref, o_ref, edge_ref, sems):
        c = core_ref[0]
        k = pl.program_id(0)
        slot = jnp.where(k < 3, slot_at(k, c), 0)
        parts = 4
        copies = []
        for p in range(parts):
            span = pl.ds(p * (width // parts), width // parts)
            for n in range(3 - CUTS):
                copies.append(pltpu.make_async_copy(e_ref.at[CUTS + n, c, span], edge_ref.at[n, span], sems.at[n * parts + p]))

        @pl.when(k == 0)
        def _():
            for copy in copies:
                copy.start()

        high, low = split((t_ref[0, 0, 0] * root(live_ref, index_ref, coef_ref, jnp.where(k < 3, c, 1 - c), slot, width)).T)
        o_ref[0, 0] = high
        o_ref[0, 1] = low

        @pl.when(k == 3)
        def _():
            for copy in copies:
                copy.wait()

    return pl.pallas_call(
        kernel,
        grid_spec=pltpu.PrefetchScalarGridSpec(
            num_scalar_prefetch=1,
            grid=(4,),
            in_specs=SCALARS + [pl.BlockSpec((1, 1, 1, width, width), lambda k, c: (0, jnp.where(k < 3, c[0], 1 - c[0]), jnp.where(k < 3, slot_at(k, c[0]), 0), 0, 0)), HBM_REF, HBM_REF],
            out_specs=[pl.BlockSpec((1, 2, width, width), lambda k, c: (jnp.where(k < 3, k, 6), 0, 0, 0)), pl.BlockSpec(memory_space=pltpu.VMEM)],
            scratch_shapes=[pltpu.SemaphoreType.DMA((4 * (3 - CUTS),))],
        ),
        out_shape=[jax.ShapeDtypeStruct((STORE, 2, width, width), BF16), jax.ShapeDtypeStruct((3 - CUTS, width, width), F32)],
        compiler_params=params(),
        cost_estimate=cost(),
        name="own_store",
    )(core, *scalars, tensors, env, after)


def full_store(store, received):
    width = store.shape[-1]

    def kernel(*refs):
        o_ref = refs[-1]
        for k in range(3):

            @pl.when(pl.program_id(0) == k)
            def _():
                high, low = split(refs[k][...].T)
                o_ref[0, 0] = high
                o_ref[0, 1] = low

    return pl.pallas_call(
        kernel,
        grid=(3,),
        in_specs=[pl.BlockSpec((width, width), lambda k: (0, 0))] * 3 + [HBM_REF],
        out_specs=pl.BlockSpec((1, 2, width, width), lambda k: (k + 3, 0, 0, 0)),
        out_shape=jax.ShapeDtypeStruct(store.shape, BF16),
        input_output_aliases={3: 0},
        compiler_params=params(),
        cost_estimate=cost(),
        name="full_store",
    )(*received, store)


def near_terms(core, site, own, other, in_env, store, parts, after):
    states, width = own.shape[0], own.shape[-1]
    rows = width // parts

    def kernel(core_ref, a_ref, b_ref, ta_ref, tb_ref, *refs):
        a, b = (a_ref[0, 0], b_ref[0, 0]) if in_env else (a_ref[0], b_ref[0])
        total = sandwich(a, ta_ref[0, 0], ta_ref[0, 1]) + sandwich(b, tb_ref[0, 0], tb_ref[0, 1])
        for p in range(parts):
            refs[len(after) + p][0] = total[p * rows : (p + 1) * rows]

    def slot(k):
        return lambda n, c: ((3 * c[0] if site == 0 else 3 - 3 * c[0]) + k, 0, 0, 0)

    row = pl.BlockSpec((1, width, width), lambda n, c: (n, 0, 0))
    sources = [row, row]
    if in_env:
        block = (1, 1, width, width)
        sources = [pl.BlockSpec(block, lambda n, c: (n, c[0], 0, 0)), pl.BlockSpec(block, lambda n, c: (n, 1 - c[0], 0, 0))]
    pair = (1, 2, width, width)
    return pl.pallas_call(
        kernel,
        grid_spec=pltpu.PrefetchScalarGridSpec(
            num_scalar_prefetch=1,
            grid=(states,),
            in_specs=sources + [pl.BlockSpec(pair, slot(0)), pl.BlockSpec(pair, slot(1))] + [HBM_REF] * len(after),
            out_specs=[pl.BlockSpec((1, rows, width), lambda n, c: (n, 0, 0))] * parts,
        ),
        out_shape=[jax.ShapeDtypeStruct((states, rows, width), F32)] * parts,
        compiler_params=params(),
        cost_estimate=cost(),
        name=f"near_terms_{site}",
    )(core, own, other, store, store, *after)


def far_terms(core, site, partial, first, halo, store, parts, weight, after):
    states, width = halo.shape[0], halo.shape[-1]
    rows = width // parts

    def kernel(core_ref, p_ref, h_ref, t_ref, *refs):
        total = p_ref[0] + sandwich(h_ref[0], t_ref[0, 0], t_ref[0, 1])
        for p in range(parts):
            refs[len(after) + p][0] = total[p * rows : (p + 1) * rows]

    return pl.pallas_call(
        kernel,
        grid_spec=pltpu.PrefetchScalarGridSpec(
            num_scalar_prefetch=1,
            grid=(states,),
            in_specs=[
                pl.BlockSpec((1, width, width), lambda n, c: (n + first, 0, 0)),
                pl.BlockSpec((1, width, width), lambda n, c: (n, 0, 0)),
                pl.BlockSpec((1, 2, width, width), lambda n, c: ((3 * c[0] if site == 0 else 3 - 3 * c[0]) + 2, 0, 0, 0)),
            ]
            + [HBM_REF] * len(after),
            out_specs=[pl.BlockSpec((1, rows, width), lambda n, c: (n, 0, 0))] * parts,
        ),
        out_shape=[jax.ShapeDtypeStruct((states, rows, width), F32)] * parts,
        compiler_params=params(),
        cost_estimate=cost(weight),
        name=f"far_terms_{site}",
    )(core, partial, halo, store, *after)


def write_rows(core, out, shape, moves, name):
    width = shape[-1]
    sources = [block for c in range(2) for blocks, _, _ in moves[c] for block in blocks]
    count = len(sources)
    old = [] if out is None else [out]

    def kernel(core_ref, *refs):
        o_ref, sems = refs[count + len(old)], refs[-1]
        if not old:
            refs[count + 1][...] = jnp.zeros((8, 128), F32)
        at = 0
        plans = []
        for c in range(2):
            plan = []
            for blocks, state, sector in moves[c]:
                rows = width // len(blocks)
                for p in range(len(blocks)):
                    plan += [(at, n, state + n, sector, p * rows, rows) for n in range(blocks[p].shape[0])]
                    at += 1
            plans.append(plan)
        for c in range(2):

            @pl.when(core_ref[0] == c)
            def _():
                copies = [
                    pltpu.make_async_copy(refs[i].at[n], o_ref.at[state, sector, pl.ds(begin, rows)], sems.at[m])
                    for m, (i, n, state, sector, begin, rows) in enumerate(plans[c])
                ]
                for copy in copies:
                    copy.start()
                for copy in copies:
                    copy.wait()

    outs = [jax.ShapeDtypeStruct(shape, F32)]
    if not old:
        outs.append(jax.ShapeDtypeStruct((8, 128), F32))
    return pl.pallas_call(
        kernel,
        grid_spec=pltpu.PrefetchScalarGridSpec(
            num_scalar_prefetch=1,
            grid=(1,),
            in_specs=[pl.BlockSpec(memory_space=pltpu.VMEM)] * count + [HBM_REF] * len(old),
            out_specs=[HBM_REF, pl.BlockSpec(memory_space=pltpu.VMEM)][: len(outs)],
            scratch_shapes=[pltpu.SemaphoreType.DMA((16,))],
        ),
        out_shape=outs,
        input_output_aliases={count + 1: 0} if old else {},
        compiler_params=params(),
        cost_estimate=cost(),
        name=name,
    )(core, *sources, *old)


def last_rows(core, out, moved, partials, sums, from_left, from_right, store):
    width = from_left.shape[-1]
    rows = width // HALVES
    first = out.shape[0] - from_left.shape[0]
    given = [*moved, *partials, *sums]
    early = moved[0].shape[1]

    def kernel(core_ref, *refs):
        blocks, near = refs[: len(moved)], refs[len(moved) : len(given)]
        left, right, t_left, t_right, _, o_ref, buf, sems, early_sems = refs[len(given) :]

        @pl.when(core_ref[0] == 1)
        def _():
            copies = []
            for p, block in enumerate(blocks):
                for n in range(first):
                    copies.append(pltpu.make_async_copy(block.at[n], o_ref.at[n, 0, pl.ds(p * early, early)], early_sems.at[p, n]))
                    copies[-1].start()
            for sector, (halo, t) in enumerate(((left, t_left), (right, t_right))):
                high, low = t[0, 0], t[0, 1]
                inner_high, inner_low = inner_halves(halo[0], high, low)
                for h in range(HALVES):
                    span = slice(h * rows, (h + 1) * rows)
                    part, inside = h * PARTS // HALVES, h * rows % (width // PARTS)
                    base = near[sector * PARTS + part][0, inside : inside + rows]
                    buf[sector, span] = base + outer(high[span], low[span], inner_high, inner_low)
                    copies.append(pltpu.make_async_copy(buf.at[sector, span], o_ref.at[first, sector, span], sems.at[sector, h]))
                    copies[-1].start()
            for copy in copies:
                copy.wait()

    whole = pl.BlockSpec(memory_space=pltpu.VMEM)
    pair = (1, 2, width, width)
    return pl.pallas_call(
        kernel,
        grid_spec=pltpu.PrefetchScalarGridSpec(
            num_scalar_prefetch=1,
            grid=(1,),
            in_specs=[whole] * (len(given) + 2)
            + [pl.BlockSpec(pair, lambda n, c: (6, 0, 0, 0)), pl.BlockSpec(pair, lambda n, c: (2, 0, 0, 0)), HBM_REF],
            out_specs=HBM_REF,
            scratch_shapes=[
                pltpu.VMEM((2, width, width), F32),
                pltpu.SemaphoreType.DMA((2, HALVES)),
                pltpu.SemaphoreType.DMA((len(moved), first)),
            ],
        ),
        out_shape=jax.ShapeDtypeStruct(out.shape, F32),
        input_output_aliases={len(given) + 5: 0},
        compiler_params=params(),
        cost_estimate=cost(),
        name="last_rows",
    )(core, *given, from_left, from_right, store, store, out)


def shards(chips, env_in, site_tensor, pair_live, coef_index, mpo_coef):
    axes = ("site", "blk")
    core = jnp.reshape(lax.axis_index("site"), (1,)).astype(jnp.int32)
    swap = [(s * chips + j, (1 - s) * chips + j) for s in range(2) for j in range(chips)]
    meet = [(chips + j, j + 1) for j in range(chips - 1)] + [(j + 1, chips + j) for j in range(chips - 1)]

    to_right = [(chips + j, chips + j + 1) for j in range(chips - 1)]
    to_left = [(j + 1, chips + j) for j in range(chips - 1)]

    def send(value, pairs):
        return lax.ppermute(value, axes, pairs)

    scalars = (pair_live, coef_index, mpo_coef)
    pinned = pltpu.with_memory_space_constraint(env_in, pltpu.HBM)
    edge_a = edge(core, pinned)
    halo_a = send(edge_a, meet)
    leaving = outgoing(core, scalars, site_tensor, edge_a)
    received = [send(block, swap) for block in leaving]
    store, edge_b = own_store(core, scalars, site_tensor, pinned, leaving[0])
    halo_b = send(edge_b, meet)
    store = full_store(store, received)

    (near,) = near_terms(core, 0, env_in, env_in, True, store, 1, [])
    (first_a,) = far_terms(core, 0, near, 0, halo_a, store, 1, 0, [])
    second_halo_a, crossed_a = send(first_a, meet), send(first_a, swap)
    (first_b,) = far_terms(core, 0, near, CUTS, halo_b, store, 1, 16, [first_a])
    from_left, from_right, crossed_b = send(first_b, to_right), send(first_b, to_left), send(first_b, swap)

    (near_a,) = near_terms(core, 1, first_a, crossed_a, False, store, 1, [])
    sums = near_terms(core, 1, first_b, crossed_b, False, store, PARTS, [near_a])
    partials = [send(block, swap) for block in sums]
    second_a = far_terms(core, 1, near_a, 0, second_halo_a, store, 2, 0, sums[:1])
    moved_a = [send(block, swap) for block in second_a]
    early = [([first_a], 0, 0), ([crossed_a], 0, 1), ([first_b], CUTS, 0), ([crossed_b], CUTS, 1)], [(second_a, 0, 1)]
    out, _ = write_rows(core, None, env_in.shape, early, "early_rows")
    out = last_rows(core, out, moved_a, partials, sums, from_left, from_right, store)
    return out[None]


def solution(mesh):
    return jax.shard_map(
        functools.partial(shards, mesh.shape["blk"]),
        mesh=mesh,
        in_specs=(
            P(None, "blk", None, None),
            P("site", "blk", None, None, None),
            P("site", "blk", None),
            P("site", "blk", None),
            P("site", None),
        ),
        out_specs=P("site", None, "blk", None, None),
        check_vma=False,
    )
```

```python
import functools

import jax
import jax.numpy as jnp
from jax import lax
from jax.experimental import pallas as pl
from jax.experimental.pallas import tpu as pltpu
from jax.sharding import PartitionSpec as P

F32 = jnp.float32
BF16 = jnp.bfloat16
LIMIT = 28 << 20

STORE = 7
CUTS = 2
SWAPS = 4
PARTS = 1
HALVES = 2


def split(x):
    high = x.astype(BF16)
    return high, (x - high.astype(F32)).astype(BF16)


def dot_nn(a, b):
    return jnp.dot(a, b, preferred_element_type=F32)


def dot_nt(a, b):
    return lax.dot_general(a, b, (((1,), (1,)), ((), ())), preferred_element_type=F32)


def inner_halves(block, high, low):
    block_high, block_low = split(block)
    return split(dot_nt(block_high, high) + dot_nt(block_high, low) + dot_nt(block_low, high))


def outer(high, low, inner_high, inner_low):
    return dot_nn(high, inner_high) + dot_nn(low, inner_high) + dot_nn(high, inner_low)


def sandwich(block, high, low):
    return outer(high, low, *inner_halves(block, high, low))


def cost(weight=0.0):
    return pl.CostEstimate(flops=int(weight * 1.15e9), bytes_accessed=1024, transcendentals=0)


def params():
    return pltpu.CompilerParams(vmem_limit_bytes=LIMIT)


def root(live_ref, index_ref, coef_ref, sector, slot, width):
    weight = live_ref[0, sector, slot].astype(F32) * coef_ref[0, index_ref[0, sector, slot]]
    return jnp.sqrt(jnp.full((1, width), weight, F32))


def slot_at(k, c):
    return jnp.where(k == 0, 1, jnp.where(k == 1, 2 - 2 * c, 2 * c))


SCALARS = [pl.BlockSpec(memory_space=pltpu.SMEM)] * 3
HBM_REF = pl.BlockSpec(memory_space=pl.ANY)


def edge(core, env):
    width = env.shape[-1]
    parts = 4
    rows = width // parts

    def kernel(core_ref, e_ref, o_ref, sems):
        copies = []
        for n in range(1):
            for p in range(parts):
                span = pl.ds(p * rows, rows)
                copies.append(pltpu.make_async_copy(e_ref.at[n, core_ref[0], span], o_ref.at[n, span], sems.at[n * parts + p]))
        for copy in copies:
            copy.start()
        for copy in copies:
            copy.wait()

    return pl.pallas_call(
        kernel,
        grid_spec=pltpu.PrefetchScalarGridSpec(
            num_scalar_prefetch=1,
            grid=(1,),
            in_specs=[HBM_REF],
            out_specs=pl.BlockSpec(memory_space=pltpu.VMEM),
            scratch_shapes=[pltpu.SemaphoreType.DMA((parts,))],
        ),
        out_shape=jax.ShapeDtypeStruct((1, width, width), F32),
        compiler_params=params(),
        cost_estimate=cost(),
        name="edge",
    )(core, env)


def outgoing(core, scalars, tensors, after):
    width = tensors.shape[-1]
    rows = width // SWAPS

    def kernel(core_ref, live_ref, index_ref, coef_ref, t_ref, after_ref, *o_refs):
        other = 1 - core_ref[0]
        for k in range(3):
            slot = slot_at(k, other)
            scaled = t_ref[0, 0, slot] * root(live_ref, index_ref, coef_ref, other, slot, width)
            for p, o_ref in enumerate(o_refs):
                o_ref[k] = scaled[p * rows : (p + 1) * rows]

    return pl.pallas_call(
        kernel,
        grid_spec=pltpu.PrefetchScalarGridSpec(
            num_scalar_prefetch=1,
            grid=(1,),
            in_specs=SCALARS + [pl.BlockSpec((1, 1, 3, width, width), lambda k, c: (0, 1 - c[0], 0, 0, 0)), HBM_REF],
            out_specs=[pl.BlockSpec((3, rows, width), lambda k, c: (0, 0, 0))] * SWAPS,
        ),
        out_shape=[jax.ShapeDtypeStruct((3, rows, width), F32)] * SWAPS,
        compiler_params=params(),
        cost_estimate=cost(),
        name="outgoing",
    )(core, *scalars, tensors, after)


def own_store(core, scalars, tensors, env, after):
    width = tensors.shape[-1]

    def kernel(core_ref, live_ref, index_ref, coef_ref, t_ref, e_ref, after_ref, o_ref, edge_ref, sems):
        c = core_ref[0]
        k = pl.program_id(0)
        slot = jnp.where(k < 3, slot_at(k, c), 0)
        parts = 4
        copies = []
        for p in range(parts):
            span = pl.ds(p * (width // parts), width // parts)
            copies.append(pltpu.make_async_copy(e_ref.at[1, c, span], edge_ref.at[0, span], sems.at[p]))

        @pl.when(k == 0)
        def _():
            for copy in copies:
                copy.start()

        high, low = split((t_ref[0, 0, 0] * root(live_ref, index_ref, coef_ref, jnp.where(k < 3, c, 1 - c), slot, width)).T)
        o_ref[0, 0] = high
        o_ref[0, 1] = low

        @pl.when(k == 3)
        def _():
            for copy in copies:
                copy.wait()

    return pl.pallas_call(
        kernel,
        grid_spec=pltpu.PrefetchScalarGridSpec(
            num_scalar_prefetch=1,
            grid=(4,),
            in_specs=SCALARS + [pl.BlockSpec((1, 1, 1, width, width), lambda k, c: (0, jnp.where(k < 3, c[0], 1 - c[0]), jnp.where(k < 3, slot_at(k, c[0]), 0), 0, 0)), HBM_REF, HBM_REF],
            out_specs=[pl.BlockSpec((1, 2, width, width), lambda k, c: (jnp.where(k < 3, k, 6), 0, 0, 0)), pl.BlockSpec(memory_space=pltpu.VMEM)],
            scratch_shapes=[pltpu.SemaphoreType.DMA((4,))],
        ),
        out_shape=[jax.ShapeDtypeStruct((STORE, 2, width, width), BF16), jax.ShapeDtypeStruct((1, width, width), F32)],
        compiler_params=params(),
        cost_estimate=cost(),
        name="own_store",
    )(core, *scalars, tensors, env, after)


def full_store(core, store, received, env):
    width = store.shape[-1]
    rows = width // SWAPS

    def kernel(core_ref, *refs):
        blocks, (_, e_ref, o_ref, edge_ref, sems) = refs[:SWAPS], refs[SWAPS:]
        k = pl.program_id(0)
        copies = []
        for p in range(SWAPS):
            span = pl.ds(p * rows, rows)
            copies.append(pltpu.make_async_copy(e_ref.at[2, core_ref[0], span], edge_ref.at[0, span], sems.at[p]))

        @pl.when(k == 0)
        def _():
            for copy in copies:
                copy.start()

        high, low = split(jnp.concatenate([block[0] for block in blocks], 0).T)
        o_ref[0, 0] = high
        o_ref[0, 1] = low

        @pl.when(k == 2)
        def _():
            for copy in copies:
                copy.wait()

    return pl.pallas_call(
        kernel,
        grid_spec=pltpu.PrefetchScalarGridSpec(
            num_scalar_prefetch=1,
            grid=(3,),
            in_specs=[pl.BlockSpec((1, rows, width), lambda k, c: (k, 0, 0))] * SWAPS + [HBM_REF, HBM_REF],
            out_specs=[pl.BlockSpec((1, 2, width, width), lambda k, c: (k + 3, 0, 0, 0)), pl.BlockSpec(memory_space=pltpu.VMEM)],
            scratch_shapes=[pltpu.SemaphoreType.DMA((SWAPS,))],
        ),
        out_shape=[jax.ShapeDtypeStruct(store.shape, BF16), jax.ShapeDtypeStruct((1, width, width), F32)],
        input_output_aliases={SWAPS + 1: 0},
        compiler_params=params(),
        cost_estimate=cost(),
        name="full_store",
    )(core, *received, store, env)


def near_terms(core, site, own, other, in_env, store, parts, after, first=0, states=None):
    states, width = states or own.shape[0], own.shape[-1]
    rows = width // parts

    def kernel(core_ref, a_ref, b_ref, ta_ref, tb_ref, *refs):
        a, b = (a_ref[0, 0], b_ref[0, 0]) if in_env else (a_ref[0], b_ref[0])
        total = sandwich(a, ta_ref[0, 0], ta_ref[0, 1]) + sandwich(b, tb_ref[0, 0], tb_ref[0, 1])
        for p in range(parts):
            refs[len(after) + p][0] = total[p * rows : (p + 1) * rows]

    def slot(k):
        return lambda n, c: ((3 * c[0] if site == 0 else 3 - 3 * c[0]) + k, 0, 0, 0)

    row = pl.BlockSpec((1, width, width), lambda n, c: (n, 0, 0))
    sources = [row, row]
    if in_env:
        block = (1, 1, width, width)
        sources = [pl.BlockSpec(block, lambda n, c: (n + first, c[0], 0, 0)), pl.BlockSpec(block, lambda n, c: (n + first, 1 - c[0], 0, 0))]
    pair = (1, 2, width, width)
    return pl.pallas_call(
        kernel,
        grid_spec=pltpu.PrefetchScalarGridSpec(
            num_scalar_prefetch=1,
            grid=(states,),
            in_specs=sources + [pl.BlockSpec(pair, slot(0)), pl.BlockSpec(pair, slot(1))] + [HBM_REF] * len(after),
            out_specs=[pl.BlockSpec((1, rows, width), lambda n, c: (n, 0, 0))] * parts,
        ),
        out_shape=[jax.ShapeDtypeStruct((states, rows, width), F32)] * parts,
        compiler_params=params(),
        cost_estimate=cost(),
        name=f"near_terms_{site}",
    )(core, own, other, store, store, *after)


def far_terms(core, site, partial, first, halo, store, parts, weight, after):
    states, width = halo.shape[0], halo.shape[-1]
    rows = width // parts

    def kernel(core_ref, p_ref, h_ref, t_ref, *refs):
        total = p_ref[0] + sandwich(h_ref[0], t_ref[0, 0], t_ref[0, 1])
        for p in range(parts):
            refs[len(after) + p][0] = total[p * rows : (p + 1) * rows]

    return pl.pallas_call(
        kernel,
        grid_spec=pltpu.PrefetchScalarGridSpec(
            num_scalar_prefetch=1,
            grid=(states,),
            in_specs=[
                pl.BlockSpec((1, width, width), lambda n, c: (n + first, 0, 0)),
                pl.BlockSpec((1, width, width), lambda n, c: (n, 0, 0)),
                pl.BlockSpec((1, 2, width, width), lambda n, c: ((3 * c[0] if site == 0 else 3 - 3 * c[0]) + 2, 0, 0, 0)),
            ]
            + [HBM_REF] * len(after),
            out_specs=[pl.BlockSpec((1, rows, width), lambda n, c: (n, 0, 0))] * parts,
        ),
        out_shape=[jax.ShapeDtypeStruct((states, rows, width), F32)] * parts,
        compiler_params=params(),
        cost_estimate=cost(weight),
        name=f"far_terms_{site}",
    )(core, partial, halo, store, *after)


def far_pair(core, partial, done, halo, store, weight):
    width = halo.shape[-1]

    def kernel(core_ref, p_ref, d_ref, h_ref, t_ref, o_ref):
        o_ref[0] = d_ref[0]
        o_ref[1] = p_ref[0] + sandwich(h_ref[0], t_ref[0, 0], t_ref[0, 1])

    row = pl.BlockSpec((1, width, width), lambda n, c: (0, 0, 0))
    return pl.pallas_call(
        kernel,
        grid_spec=pltpu.PrefetchScalarGridSpec(
            num_scalar_prefetch=1,
            grid=(1,),
            in_specs=[
                pl.BlockSpec((1, width, width), lambda n, c: (1, 0, 0)),
                row,
                row,
                pl.BlockSpec((1, 2, width, width), lambda n, c: (3 * c[0] + 2, 0, 0, 0)),
            ],
            out_specs=pl.BlockSpec((2, width, width), lambda n, c: (0, 0, 0)),
        ),
        out_shape=jax.ShapeDtypeStruct((2, width, width), F32),
        compiler_params=params(),
        cost_estimate=cost(weight),
        name="far_pair",
    )(core, partial, done, halo, store)


def write_rows(core, out, shape, moves, name):
    width = shape[-1]
    sources = [block for c in range(2) for blocks, _, _ in moves[c] for block in blocks]
    count = len(sources)
    old = [] if out is None else [out]

    def kernel(core_ref, *refs):
        o_ref, sems = refs[count + len(old)], refs[-1]
        if not old:
            refs[count + 1][...] = jnp.zeros((8, 128), F32)
        at = 0
        plans = []
        for c in range(2):
            plan = []
            for blocks, state, sector in moves[c]:
                rows = width // len(blocks)
                for p in range(len(blocks)):
                    plan += [(at, n, state + n, sector, p * rows, rows) for n in range(blocks[p].shape[0])]
                    at += 1
            plans.append(plan)
        for c in range(2):

            @pl.when(core_ref[0] == c)
            def _():
                copies = [
                    pltpu.make_async_copy(refs[i].at[n], o_ref.at[state, sector, pl.ds(begin, rows)], sems.at[m])
                    for m, (i, n, state, sector, begin, rows) in enumerate(plans[c])
                ]
                for copy in copies:
                    copy.start()
                for copy in copies:
                    copy.wait()

    outs = [jax.ShapeDtypeStruct(shape, F32)]
    if not old:
        outs.append(jax.ShapeDtypeStruct((8, 128), F32))
    return pl.pallas_call(
        kernel,
        grid_spec=pltpu.PrefetchScalarGridSpec(
            num_scalar_prefetch=1,
            grid=(1,),
            in_specs=[pl.BlockSpec(memory_space=pltpu.VMEM)] * count + [HBM_REF] * len(old),
            out_specs=[HBM_REF, pl.BlockSpec(memory_space=pltpu.VMEM)][: len(outs)],
            scratch_shapes=[pltpu.SemaphoreType.DMA((16,))],
        ),
        out_shape=outs,
        input_output_aliases={count + 1: 0} if old else {},
        compiler_params=params(),
        cost_estimate=cost(),
        name=name,
    )(core, *sources, *old)


def last_rows(core, out, moved, partials, sums, from_left, from_right, store):
    width = from_left.shape[-1]
    rows = width // HALVES
    first = out.shape[0] - from_left.shape[0]
    given = [*moved, *partials, *sums]
    early = moved[0].shape[1]

    def kernel(core_ref, *refs):
        blocks, near = refs[: len(moved)], refs[len(moved) : len(given)]
        left, right, t_left, t_right, _, o_ref, buf, sems, early_sems = refs[len(given) :]

        @pl.when(core_ref[0] == 1)
        def _():
            copies = []
            for p, block in enumerate(blocks):
                for n in range(first):
                    copies.append(pltpu.make_async_copy(block.at[n], o_ref.at[n, 0, pl.ds(p * early, early)], early_sems.at[p, n]))
                    copies[-1].start()
            for sector, (halo, t) in enumerate(((left, t_left), (right, t_right))):
                high, low = t[0, 0], t[0, 1]
                inner_high, inner_low = inner_halves(halo[0], high, low)
                for h in range(HALVES):
                    span = slice(h * rows, (h + 1) * rows)
                    part, inside = h * PARTS // HALVES, h * rows % (width // PARTS)
                    base = near[sector * PARTS + part][0, inside : inside + rows]
                    buf[sector, span] = base + outer(high[span], low[span], inner_high, inner_low)
                    copies.append(pltpu.make_async_copy(buf.at[sector, span], o_ref.at[first, sector, span], sems.at[sector, h]))
                    copies[-1].start()
            for copy in copies:
                copy.wait()

    whole = pl.BlockSpec(memory_space=pltpu.VMEM)
    pair = (1, 2, width, width)
    return pl.pallas_call(
        kernel,
        grid_spec=pltpu.PrefetchScalarGridSpec(
            num_scalar_prefetch=1,
            grid=(1,),
            in_specs=[whole] * (len(given) + 2)
            + [pl.BlockSpec(pair, lambda n, c: (6, 0, 0, 0)), pl.BlockSpec(pair, lambda n, c: (2, 0, 0, 0)), HBM_REF],
            out_specs=HBM_REF,
            scratch_shapes=[
                pltpu.VMEM((2, width, width), F32),
                pltpu.SemaphoreType.DMA((2, HALVES)),
                pltpu.SemaphoreType.DMA((len(moved), first)),
            ],
        ),
        out_shape=jax.ShapeDtypeStruct(out.shape, F32),
        input_output_aliases={len(given) + 5: 0},
        compiler_params=params(),
        cost_estimate=cost(),
        name="last_rows",
    )(core, *given, from_left, from_right, store, store, out)


def shards(chips, env_in, site_tensor, pair_live, coef_index, mpo_coef):
    axes = ("site", "blk")
    core = jnp.reshape(lax.axis_index("site"), (1,)).astype(jnp.int32)
    swap = [(s * chips + j, (1 - s) * chips + j) for s in range(2) for j in range(chips)]
    meet = [(chips + j, j + 1) for j in range(chips - 1)] + [(j + 1, chips + j) for j in range(chips - 1)]

    to_right = [(chips + j, chips + j + 1) for j in range(chips - 1)]
    to_left = [(j + 1, chips + j) for j in range(chips - 1)]

    def send(value, pairs):
        return lax.ppermute(value, axes, pairs)

    scalars = (pair_live, coef_index, mpo_coef)
    pinned = pltpu.with_memory_space_constraint(env_in, pltpu.HBM)
    edge_0 = edge(core, pinned)
    halo_0 = send(edge_0, meet)
    leaving = outgoing(core, scalars, site_tensor, edge_0)
    received = [send(block, swap) for block in leaving]
    store, edge_1 = own_store(core, scalars, site_tensor, pinned, leaving[0])
    halo_1 = send(edge_1, meet)
    store, edge_2 = full_store(core, store, received, pinned)
    halo_2 = send(edge_2, meet)

    (near_01,) = near_terms(core, 0, env_in, env_in, True, store, 1, [], 0, CUTS)
    (first_0,) = far_terms(core, 0, near_01, 0, halo_0, store, 1, 16, [])
    first_a = far_pair(core, near_01, first_0, halo_1, store, 0)
    second_halo_a, crossed_a = send(first_a, meet), send(first_a, swap)
    (near_2,) = near_terms(core, 0, env_in, env_in, True, store, 1, [first_a], CUTS, 3 - CUTS)
    (first_b,) = far_terms(core, 0, near_2, 0, halo_2, store, 1, 0, [first_a])
    from_left, from_right, crossed_b = send(first_b, to_right), send(first_b, to_left), send(first_b, swap)

    (near_a,) = near_terms(core, 1, first_a, crossed_a, False, store, 1, [])
    sums = near_terms(core, 1, first_b, crossed_b, False, store, PARTS, [near_a])
    partials = [send(block, swap) for block in sums]
    second_a = far_terms(core, 1, near_a, 0, second_halo_a, store, 2, 0, sums[:1])
    moved_a = [send(block, swap) for block in second_a]
    early = [([first_a], 0, 0), ([crossed_a], 0, 1), ([first_b], CUTS, 0), ([crossed_b], CUTS, 1)], [(second_a, 0, 1)]
    out, _ = write_rows(core, None, env_in.shape, early, "early_rows")
    out = last_rows(core, out, moved_a, partials, sums, from_left, from_right, store)
    return out[None]


def solution(mesh):
    return jax.shard_map(
        functools.partial(shards, mesh.shape["blk"]),
        mesh=mesh,
        in_specs=(
            P(None, "blk", None, None),
            P("site", "blk", None, None, None),
            P("site", "blk", None),
            P("site", "blk", None),
            P("site", None),
        ),
        out_specs=P("site", None, "blk", None, None),
        check_vma=False,
    )
```

```python
import functools

import jax
import jax.numpy as jnp
from jax import lax
from jax.experimental import pallas as pl
from jax.experimental.pallas import tpu as pltpu
from jax.sharding import PartitionSpec as P

F32 = jnp.float32
BF16 = jnp.bfloat16
LIMIT = 28 << 20

STORE = 7
CUTS = 2
SWAPS = 4
PARTS = 1
HALVES = 2


def split(x):
    high = x.astype(BF16)
    return high, (x - high.astype(F32)).astype(BF16)


def dot_nn(a, b):
    return jnp.dot(a, b, preferred_element_type=F32)


def dot_nt(a, b):
    return lax.dot_general(a, b, (((1,), (1,)), ((), ())), preferred_element_type=F32)


def inner_halves(block, high, low):
    block_high, block_low = split(block)
    return split(dot_nt(block_high, high) + dot_nt(block_high, low) + dot_nt(block_low, high))


def outer(high, low, inner_high, inner_low):
    return dot_nn(high, inner_high) + dot_nn(low, inner_high) + dot_nn(high, inner_low)


def sandwich(block, high, low):
    return outer(high, low, *inner_halves(block, high, low))


def cost(weight=0.0):
    return pl.CostEstimate(flops=int(weight * 1.15e9), bytes_accessed=1024, transcendentals=0)


def params():
    return pltpu.CompilerParams(vmem_limit_bytes=LIMIT)


def root(live_ref, index_ref, coef_ref, sector, slot, width):
    weight = live_ref[0, sector, slot].astype(F32) * coef_ref[0, index_ref[0, sector, slot]]
    return jnp.sqrt(jnp.full((1, width), weight, F32))


def slot_at(k, c):
    return jnp.where(k == 0, 1, jnp.where(k == 1, 2 - 2 * c, 2 * c))


SCALARS = [pl.BlockSpec(memory_space=pltpu.SMEM)] * 3
HBM_REF = pl.BlockSpec(memory_space=pl.ANY)


def edge(core, env):
    width = env.shape[-1]
    parts = 4
    rows = width // parts

    def kernel(core_ref, e_ref, o_ref, sems):
        copies = []
        for n in range(1):
            for p in range(parts):
                span = pl.ds(p * rows, rows)
                copies.append(pltpu.make_async_copy(e_ref.at[n, core_ref[0], span], o_ref.at[n, span], sems.at[n * parts + p]))
        for copy in copies:
            copy.start()
        for copy in copies:
            copy.wait()

    return pl.pallas_call(
        kernel,
        grid_spec=pltpu.PrefetchScalarGridSpec(
            num_scalar_prefetch=1,
            grid=(1,),
            in_specs=[HBM_REF],
            out_specs=pl.BlockSpec(memory_space=pltpu.VMEM),
            scratch_shapes=[pltpu.SemaphoreType.DMA((parts,))],
        ),
        out_shape=jax.ShapeDtypeStruct((1, width, width), F32),
        compiler_params=params(),
        cost_estimate=cost(),
        name="edge",
    )(core, env)


def outgoing(core, scalars, tensors, after):
    width = tensors.shape[-1]
    rows = width // SWAPS

    def kernel(core_ref, live_ref, index_ref, coef_ref, t_ref, after_ref, *o_refs):
        other = 1 - core_ref[0]
        for k in range(3):
            slot = slot_at(k, other)
            scaled = t_ref[0, 0, slot] * root(live_ref, index_ref, coef_ref, other, slot, width)
            for p, o_ref in enumerate(o_refs):
                o_ref[k] = scaled[p * rows : (p + 1) * rows]

    return pl.pallas_call(
        kernel,
        grid_spec=pltpu.PrefetchScalarGridSpec(
            num_scalar_prefetch=1,
            grid=(1,),
            in_specs=SCALARS + [pl.BlockSpec((1, 1, 3, width, width), lambda k, c: (0, 1 - c[0], 0, 0, 0)), HBM_REF],
            out_specs=[pl.BlockSpec((3, rows, width), lambda k, c: (0, 0, 0))] * SWAPS,
        ),
        out_shape=[jax.ShapeDtypeStruct((3, rows, width), F32)] * SWAPS,
        compiler_params=params(),
        cost_estimate=cost(),
        name="outgoing",
    )(core, *scalars, tensors, after)


def own_store(core, scalars, tensors, env, after):
    width = tensors.shape[-1]

    def kernel(core_ref, live_ref, index_ref, coef_ref, t_ref, e_ref, after_ref, o_ref, edge_ref, sems):
        c = core_ref[0]
        k = pl.program_id(0)
        slot = jnp.where(k < 3, slot_at(k, c), 0)
        parts = 4
        copies = []
        for p in range(parts):
            span = pl.ds(p * (width // parts), width // parts)
            copies.append(pltpu.make_async_copy(e_ref.at[1, c, span], edge_ref.at[0, span], sems.at[p]))

        @pl.when(k == 0)
        def _():
            for copy in copies:
                copy.start()

        high, low = split((t_ref[0, 0, 0] * root(live_ref, index_ref, coef_ref, jnp.where(k < 3, c, 1 - c), slot, width)).T)
        o_ref[0, 0] = high
        o_ref[0, 1] = low

        @pl.when(k == 3)
        def _():
            for copy in copies:
                copy.wait()

    return pl.pallas_call(
        kernel,
        grid_spec=pltpu.PrefetchScalarGridSpec(
            num_scalar_prefetch=1,
            grid=(4,),
            in_specs=SCALARS + [pl.BlockSpec((1, 1, 1, width, width), lambda k, c: (0, jnp.where(k < 3, c[0], 1 - c[0]), jnp.where(k < 3, slot_at(k, c[0]), 0), 0, 0)), HBM_REF, HBM_REF],
            out_specs=[pl.BlockSpec((1, 2, width, width), lambda k, c: (jnp.where(k < 3, k, 6), 0, 0, 0)), pl.BlockSpec(memory_space=pltpu.VMEM)],
            scratch_shapes=[pltpu.SemaphoreType.DMA((4,))],
        ),
        out_shape=[jax.ShapeDtypeStruct((STORE, 2, width, width), BF16), jax.ShapeDtypeStruct((1, width, width), F32)],
        compiler_params=params(),
        cost_estimate=cost(),
        name="own_store",
    )(core, *scalars, tensors, env, after)


def full_store(core, store, received, env):
    width = store.shape[-1]
    rows = width // SWAPS

    def kernel(core_ref, *refs):
        blocks, (_, e_ref, o_ref, edge_ref, sems) = refs[:SWAPS], refs[SWAPS:]
        k = pl.program_id(0)
        copies = []
        for p in range(SWAPS):
            span = pl.ds(p * rows, rows)
            copies.append(pltpu.make_async_copy(e_ref.at[2, core_ref[0], span], edge_ref.at[0, span], sems.at[p]))

        @pl.when(k == 0)
        def _():
            for copy in copies:
                copy.start()

        high, low = split(jnp.concatenate([block[0] for block in blocks], 0).T)
        o_ref[0, 0] = high
        o_ref[0, 1] = low

        @pl.when(k == 2)
        def _():
            for copy in copies:
                copy.wait()

    return pl.pallas_call(
        kernel,
        grid_spec=pltpu.PrefetchScalarGridSpec(
            num_scalar_prefetch=1,
            grid=(3,),
            in_specs=[pl.BlockSpec((1, rows, width), lambda k, c: (k, 0, 0))] * SWAPS + [HBM_REF, HBM_REF],
            out_specs=[pl.BlockSpec((1, 2, width, width), lambda k, c: (k + 3, 0, 0, 0)), pl.BlockSpec(memory_space=pltpu.VMEM)],
            scratch_shapes=[pltpu.SemaphoreType.DMA((SWAPS,))],
        ),
        out_shape=[jax.ShapeDtypeStruct(store.shape, BF16), jax.ShapeDtypeStruct((1, width, width), F32)],
        input_output_aliases={SWAPS + 1: 0},
        compiler_params=params(),
        cost_estimate=cost(),
        name="full_store",
    )(core, *received, store, env)


def near_terms(core, site, own, other, in_env, store, parts, after, first=0, states=None):
    states, width = states or own.shape[0], own.shape[-1]
    rows = width // parts

    def kernel(core_ref, a_ref, b_ref, ta_ref, tb_ref, *refs):
        a, b = (a_ref[0, 0], b_ref[0, 0]) if in_env else (a_ref[0], b_ref[0])
        total = sandwich(a, ta_ref[0, 0], ta_ref[0, 1]) + sandwich(b, tb_ref[0, 0], tb_ref[0, 1])
        for p in range(parts):
            refs[len(after) + p][0] = total[p * rows : (p + 1) * rows]

    def slot(k):
        return lambda n, c: ((3 * c[0] if site == 0 else 3 - 3 * c[0]) + k, 0, 0, 0)

    row = pl.BlockSpec((1, width, width), lambda n, c: (n, 0, 0))
    sources = [row, row]
    if in_env:
        block = (1, 1, width, width)
        sources = [pl.BlockSpec(block, lambda n, c: (n + first, c[0], 0, 0)), pl.BlockSpec(block, lambda n, c: (n + first, 1 - c[0], 0, 0))]
    pair = (1, 2, width, width)
    return pl.pallas_call(
        kernel,
        grid_spec=pltpu.PrefetchScalarGridSpec(
            num_scalar_prefetch=1,
            grid=(states,),
            in_specs=sources + [pl.BlockSpec(pair, slot(0)), pl.BlockSpec(pair, slot(1))] + [HBM_REF] * len(after),
            out_specs=[pl.BlockSpec((1, rows, width), lambda n, c: (n, 0, 0))] * parts,
        ),
        out_shape=[jax.ShapeDtypeStruct((states, rows, width), F32)] * parts,
        compiler_params=params(),
        cost_estimate=cost(),
        name=f"near_terms_{site}",
    )(core, own, other, store, store, *after)


def far_terms(core, site, partial, first, halo, store, parts, weight, after):
    states, width = halo.shape[0], halo.shape[-1]
    rows = width // parts

    def kernel(core_ref, p_ref, h_ref, t_ref, *refs):
        total = p_ref[0] + sandwich(h_ref[0], t_ref[0, 0], t_ref[0, 1])
        for p in range(parts):
            refs[len(after) + p][0] = total[p * rows : (p + 1) * rows]

    return pl.pallas_call(
        kernel,
        grid_spec=pltpu.PrefetchScalarGridSpec(
            num_scalar_prefetch=1,
            grid=(states,),
            in_specs=[
                pl.BlockSpec((1, width, width), lambda n, c: (n + first, 0, 0)),
                pl.BlockSpec((1, width, width), lambda n, c: (n, 0, 0)),
                pl.BlockSpec((1, 2, width, width), lambda n, c: ((3 * c[0] if site == 0 else 3 - 3 * c[0]) + 2, 0, 0, 0)),
            ]
            + [HBM_REF] * len(after),
            out_specs=[pl.BlockSpec((1, rows, width), lambda n, c: (n, 0, 0))] * parts,
        ),
        out_shape=[jax.ShapeDtypeStruct((states, rows, width), F32)] * parts,
        compiler_params=params(),
        cost_estimate=cost(weight),
        name=f"far_terms_{site}",
    )(core, partial, halo, store, *after)


def far_pair(core, partial, done, halo, store, weight):
    width = halo.shape[-1]

    def kernel(core_ref, p_ref, d_ref, h_ref, t_ref, o_ref):
        o_ref[0] = d_ref[0]
        o_ref[1] = p_ref[0] + sandwich(h_ref[0], t_ref[0, 0], t_ref[0, 1])

    row = pl.BlockSpec((1, width, width), lambda n, c: (0, 0, 0))
    return pl.pallas_call(
        kernel,
        grid_spec=pltpu.PrefetchScalarGridSpec(
            num_scalar_prefetch=1,
            grid=(1,),
            in_specs=[
                pl.BlockSpec((1, width, width), lambda n, c: (1, 0, 0)),
                row,
                row,
                pl.BlockSpec((1, 2, width, width), lambda n, c: (3 * c[0] + 2, 0, 0, 0)),
            ],
            out_specs=pl.BlockSpec((2, width, width), lambda n, c: (0, 0, 0)),
        ),
        out_shape=jax.ShapeDtypeStruct((2, width, width), F32),
        compiler_params=params(),
        cost_estimate=cost(weight),
        name="far_pair",
    )(core, partial, done, halo, store)


def write_rows(core, out, shape, moves, name):
    width = shape[-1]
    sources = [block for c in range(2) for blocks, _, _ in moves[c] for block in blocks]
    count = len(sources)
    old = [] if out is None else [out]

    def kernel(core_ref, *refs):
        o_ref, sems = refs[count + len(old)], refs[-1]
        if not old:
            refs[count + 1][...] = jnp.zeros((8, 128), F32)
        at = 0
        plans = []
        for c in range(2):
            plan = []
            for blocks, state, sector in moves[c]:
                rows = width // len(blocks)
                for p in range(len(blocks)):
                    plan += [(at, n, state + n, sector, p * rows, rows) for n in range(blocks[p].shape[0])]
                    at += 1
            plans.append(plan)
        for c in range(2):

            @pl.when(core_ref[0] == c)
            def _():
                copies = [
                    pltpu.make_async_copy(refs[i].at[n], o_ref.at[state, sector, pl.ds(begin, rows)], sems.at[m])
                    for m, (i, n, state, sector, begin, rows) in enumerate(plans[c])
                ]
                for copy in copies:
                    copy.start()
                for copy in copies:
                    copy.wait()

    outs = [jax.ShapeDtypeStruct(shape, F32)]
    if not old:
        outs.append(jax.ShapeDtypeStruct((8, 128), F32))
    return pl.pallas_call(
        kernel,
        grid_spec=pltpu.PrefetchScalarGridSpec(
            num_scalar_prefetch=1,
            grid=(1,),
            in_specs=[pl.BlockSpec(memory_space=pltpu.VMEM)] * count + [HBM_REF] * len(old),
            out_specs=[HBM_REF, pl.BlockSpec(memory_space=pltpu.VMEM)][: len(outs)],
            scratch_shapes=[pltpu.SemaphoreType.DMA((16,))],
        ),
        out_shape=outs,
        input_output_aliases={count + 1: 0} if old else {},
        compiler_params=params(),
        cost_estimate=cost(),
        name=name,
    )(core, *sources, *old)


RING = 4


def sooner(j):
    return (lax.rem(j, RING) == 0) * 1 if isinstance(j, jax.Array) else int(j % RING == 0)


def sooner_term(core, halo, store, after):
    width = halo.shape[-1]

    def kernel(core_ref, h_ref, t_ref, after_ref, o_ref):
        @pl.when(core_ref[0] == 1)
        def _():
            slot = 6 - 4 * sooner(lax.axis_index("blk"))
            o_ref[...] = sandwich(h_ref[0], t_ref[slot, 0], t_ref[slot, 1])

    return pl.pallas_call(
        kernel,
        grid_spec=pltpu.PrefetchScalarGridSpec(
            num_scalar_prefetch=1,
            grid=(1,),
            in_specs=[
                pl.BlockSpec((1, width, width), lambda n, c: (0, 0, 0)),
                pl.BlockSpec(memory_space=pltpu.VMEM),
                HBM_REF,
            ],
            out_specs=pl.BlockSpec((width, width), lambda n, c: (0, 0)),
        ),
        out_shape=jax.ShapeDtypeStruct((width, width), F32),
        compiler_params=params(),
        cost_estimate=cost(),
        name="sooner_term",
    )(core, halo, store, after)


def last_rows(core, out, moved, partial, near, sooner_far, halo, store):
    width = halo.shape[-1]
    rows = width // HALVES
    first = out.shape[0] - halo.shape[0]
    early = moved[0].shape[1]

    def kernel(core_ref, *refs):
        blocks, (partial_ref, near_ref, s_ref, h_ref, t_ref, _, o_ref, buf, sems, early_sems) = refs[: len(moved)], refs[len(moved) :]
        sector = sooner(lax.axis_index("blk"))

        def near_sum(chosen, span):
            return jnp.where(chosen == 0, partial_ref[0, span], near_ref[0, span])

        @pl.when(core_ref[0] == 1)
        def _():
            copies = []
            for p, block in enumerate(blocks):
                for n in range(first):
                    copies.append(pltpu.make_async_copy(block.at[n], o_ref.at[n, 0, pl.ds(p * early, early)], early_sems.at[p, n]))
                    copies[-1].start()
            buf[0] = s_ref[...] + near_sum(sector, slice(0, width))
            copies.append(pltpu.make_async_copy(buf.at[0], o_ref.at[first, sector], sems.at[HALVES]))
            copies[-1].start()
            slot = 2 + 4 * sector
            high, low = t_ref[slot, 0], t_ref[slot, 1]
            inner_high, inner_low = inner_halves(h_ref[0], high, low)
            for h in range(HALVES):
                span = slice(h * rows, (h + 1) * rows)
                buf[1, span] = near_sum(1 - sector, span) + outer(high[span], low[span], inner_high, inner_low)
                copies.append(pltpu.make_async_copy(buf.at[1, span], o_ref.at[first, 1 - sector, span], sems.at[h]))
                copies[-1].start()
            for copy in copies:
                copy.wait()

    whole = pl.BlockSpec(memory_space=pltpu.VMEM)
    count = len(moved) + 4
    return pl.pallas_call(
        kernel,
        grid_spec=pltpu.PrefetchScalarGridSpec(
            num_scalar_prefetch=1,
            grid=(1,),
            in_specs=[whole] * count + [whole, HBM_REF],
            out_specs=HBM_REF,
            scratch_shapes=[
                pltpu.VMEM((2, width, width), F32),
                pltpu.SemaphoreType.DMA((HALVES + 1,)),
                pltpu.SemaphoreType.DMA((len(moved), first)),
            ],
        ),
        out_shape=jax.ShapeDtypeStruct(out.shape, F32),
        input_output_aliases={count + 2: 0},
        compiler_params=params(),
        cost_estimate=cost(),
        name="last_rows",
    )(core, *moved, partial, near, sooner_far, halo, store, out)


def shards(chips, env_in, site_tensor, pair_live, coef_index, mpo_coef):
    axes = ("site", "blk")
    core = jnp.reshape(lax.axis_index("site"), (1,)).astype(jnp.int32)
    swap = [(s * chips + j, (1 - s) * chips + j) for s in range(2) for j in range(chips)]
    meet = [(chips + j, j + 1) for j in range(chips - 1)] + [(j + 1, chips + j) for j in range(chips - 1)]

    from_left = {j: (chips + j - 1, chips + j) for j in range(1, chips)}
    from_right = {j: (j + 1, chips + j) for j in range(chips - 1)}
    sides = from_left, from_right
    soon = [sides[sooner(j)][j] for j in range(chips) if j in sides[sooner(j)]]
    later = [sides[1 - sooner(j)][j] for j in range(chips) if j in sides[1 - sooner(j)]]

    def send(value, pairs):
        return lax.ppermute(value, axes, pairs)

    scalars = (pair_live, coef_index, mpo_coef)
    pinned = pltpu.with_memory_space_constraint(env_in, pltpu.HBM)
    edge_0 = edge(core, pinned)
    halo_0 = send(edge_0, meet)
    leaving = outgoing(core, scalars, site_tensor, edge_0)
    received = [send(block, swap) for block in leaving]
    store, edge_1 = own_store(core, scalars, site_tensor, pinned, leaving[0])
    halo_1 = send(edge_1, meet)
    store, edge_2 = full_store(core, store, received, pinned)
    halo_2 = send(edge_2, meet)

    (near_01,) = near_terms(core, 0, env_in, env_in, True, store, 1, [], 0, CUTS)
    (first_0,) = far_terms(core, 0, near_01, 0, halo_0, store, 1, 16, [])
    first_a = far_pair(core, near_01, first_0, halo_1, store, 0)
    second_halo_a, crossed_a = send(first_a, meet), send(first_a, swap)
    (near_2,) = near_terms(core, 0, env_in, env_in, True, store, 1, [first_a], CUTS, 3 - CUTS)
    (first_b,) = far_terms(core, 0, near_2, 0, halo_2, store, 1, 0, [first_a])
    halo_soon, halo_later, crossed_b = send(first_b, soon), send(first_b, later), send(first_b, swap)

    (near_a,) = near_terms(core, 1, first_a, crossed_a, False, store, 1, [])
    sums = near_terms(core, 1, first_b, crossed_b, False, store, PARTS, [near_a])
    partials = [send(block, swap) for block in sums]
    second_a = far_terms(core, 1, near_a, 0, second_halo_a, store, 2, 0, sums[:1])
    moved_a = [send(block, swap) for block in second_a]
    early = [([first_a], 0, 0), ([crossed_a], 0, 1), ([first_b], CUTS, 0), ([crossed_b], CUTS, 1)], [(second_a, 0, 1)]
    out, mark = write_rows(core, None, env_in.shape, early, "early_rows")
    sooner_far = sooner_term(core, halo_soon, store, mark)
    out = last_rows(core, out, moved_a, *partials, *sums, sooner_far, halo_later, store)
    return out[None]


def solution(mesh):
    return jax.shard_map(
        functools.partial(shards, mesh.shape["blk"]),
        mesh=mesh,
        in_specs=(
            P(None, "blk", None, None),
            P("site", "blk", None, None, None),
            P("site", "blk", None),
            P("site", "blk", None),
            P("site", None),
        ),
        out_specs=P("site", None, "blk", None, None),
        check_vma=False,
    )
```

```python
import functools

import jax
import jax.numpy as jnp
from jax import lax
from jax.experimental import pallas as pl
from jax.experimental.pallas import tpu as pltpu
from jax.sharding import PartitionSpec as P

F32 = jnp.float32
BF16 = jnp.bfloat16
LIMIT = 28 << 20

STORE = 7
CUTS = 2
SWAPS = 4
PARTS = 1
HALVES = 2


def split(x):
    high = x.astype(BF16)
    return high, (x - high.astype(F32)).astype(BF16)


def dot_nn(a, b):
    return jnp.dot(a, b, preferred_element_type=F32)


def dot_nt(a, b):
    return lax.dot_general(a, b, (((1,), (1,)), ((), ())), preferred_element_type=F32)


def inner_halves(block, high, low):
    block_high, block_low = split(block)
    return split(dot_nt(block_high, high) + dot_nt(block_high, low) + dot_nt(block_low, high))


def outer(high, low, inner_high, inner_low):
    return dot_nn(high, inner_high) + dot_nn(low, inner_high) + dot_nn(high, inner_low)


def sandwich(block, high, low):
    return outer(high, low, *inner_halves(block, high, low))


def cost(weight=0.0):
    return pl.CostEstimate(flops=int(weight * 1.15e9), bytes_accessed=1024, transcendentals=0)


def params():
    return pltpu.CompilerParams(vmem_limit_bytes=LIMIT)


def root(live_ref, index_ref, coef_ref, sector, slot, width):
    weight = live_ref[0, sector, slot].astype(F32) * coef_ref[0, index_ref[0, sector, slot]]
    return jnp.sqrt(jnp.full((1, width), weight, F32))


def slot_at(k, c):
    return jnp.where(k == 0, 1, jnp.where(k == 1, 2 - 2 * c, 2 * c))


SCALARS = [pl.BlockSpec(memory_space=pltpu.SMEM)] * 3
HBM_REF = pl.BlockSpec(memory_space=pl.ANY)


def edge(core, env):
    width = env.shape[-1]
    parts = 8
    rows = width // parts

    def kernel(core_ref, e_ref, o_ref, sems):
        copies = []
        for n in range(1):
            for p in range(parts):
                span = pl.ds(p * rows, rows)
                copies.append(pltpu.make_async_copy(e_ref.at[n, core_ref[0], span], o_ref.at[n, span], sems.at[n * parts + p]))
        for copy in copies:
            copy.start()
        for copy in copies:
            copy.wait()

    return pl.pallas_call(
        kernel,
        grid_spec=pltpu.PrefetchScalarGridSpec(
            num_scalar_prefetch=1,
            grid=(1,),
            in_specs=[HBM_REF],
            out_specs=pl.BlockSpec(memory_space=pltpu.VMEM),
            scratch_shapes=[pltpu.SemaphoreType.DMA((parts,))],
        ),
        out_shape=jax.ShapeDtypeStruct((1, width, width), F32),
        compiler_params=params(),
        cost_estimate=cost(),
        name="edge",
    )(core, env)


def outgoing(core, scalars, tensors, after):
    width = tensors.shape[-1]
    rows = width // SWAPS

    def kernel(core_ref, live_ref, index_ref, coef_ref, t_ref, after_ref, *o_refs):
        other = 1 - core_ref[0]
        for k in range(3):
            slot = slot_at(k, other)
            scaled = t_ref[0, 0, slot] * root(live_ref, index_ref, coef_ref, other, slot, width)
            for p, o_ref in enumerate(o_refs):
                o_ref[k] = scaled[p * rows : (p + 1) * rows]

    return pl.pallas_call(
        kernel,
        grid_spec=pltpu.PrefetchScalarGridSpec(
            num_scalar_prefetch=1,
            grid=(1,),
            in_specs=SCALARS + [pl.BlockSpec((1, 1, 3, width, width), lambda k, c: (0, 1 - c[0], 0, 0, 0)), HBM_REF],
            out_specs=[pl.BlockSpec((3, rows, width), lambda k, c: (0, 0, 0))] * SWAPS,
        ),
        out_shape=[jax.ShapeDtypeStruct((3, rows, width), F32)] * SWAPS,
        compiler_params=params(),
        cost_estimate=cost(),
        name="outgoing",
    )(core, *scalars, tensors, after)


def own_store(core, scalars, tensors, env, after):
    width = tensors.shape[-1]

    def kernel(core_ref, live_ref, index_ref, coef_ref, t_ref, e_ref, after_ref, o_ref, edge_ref, sems):
        c = core_ref[0]
        k = pl.program_id(0)
        slot = jnp.where(k < 3, slot_at(k, c), 0)
        parts = 4
        copies = []
        for p in range(parts):
            span = pl.ds(p * (width // parts), width // parts)
            copies.append(pltpu.make_async_copy(e_ref.at[1, c, span], edge_ref.at[0, span], sems.at[p]))

        @pl.when(k == 0)
        def _():
            for copy in copies:
                copy.start()

        high, low = split((t_ref[0, 0, 0] * root(live_ref, index_ref, coef_ref, jnp.where(k < 3, c, 1 - c), slot, width)).T)
        o_ref[0, 0] = high
        o_ref[0, 1] = low

        @pl.when(k == 3)
        def _():
            for copy in copies:
                copy.wait()

    return pl.pallas_call(
        kernel,
        grid_spec=pltpu.PrefetchScalarGridSpec(
            num_scalar_prefetch=1,
            grid=(4,),
            in_specs=SCALARS + [pl.BlockSpec((1, 1, 1, width, width), lambda k, c: (0, jnp.where(k < 3, c[0], 1 - c[0]), jnp.where(k < 3, slot_at(k, c[0]), 0), 0, 0)), HBM_REF, HBM_REF],
            out_specs=[pl.BlockSpec((1, 2, width, width), lambda k, c: (jnp.where(k < 3, k, 6), 0, 0, 0)), pl.BlockSpec(memory_space=pltpu.VMEM)],
            scratch_shapes=[pltpu.SemaphoreType.DMA((4,))],
        ),
        out_shape=[jax.ShapeDtypeStruct((STORE, 2, width, width), BF16), jax.ShapeDtypeStruct((1, width, width), F32)],
        compiler_params=params(),
        cost_estimate=cost(),
        name="own_store",
    )(core, *scalars, tensors, env, after)


def full_store(core, store, received, env):
    width = store.shape[-1]
    rows = width // SWAPS

    def kernel(core_ref, *refs):
        blocks, (_, e_ref, o_ref, edge_ref, sems) = refs[:SWAPS], refs[SWAPS:]
        k = pl.program_id(0)
        copies = []
        for p in range(SWAPS):
            span = pl.ds(p * rows, rows)
            copies.append(pltpu.make_async_copy(e_ref.at[2, core_ref[0], span], edge_ref.at[0, span], sems.at[p]))

        @pl.when(k == 0)
        def _():
            for copy in copies:
                copy.start()

        high, low = split(jnp.concatenate([block[0] for block in blocks], 0).T)
        o_ref[0, 0] = high
        o_ref[0, 1] = low

        @pl.when(k == 2)
        def _():
            for copy in copies:
                copy.wait()

    return pl.pallas_call(
        kernel,
        grid_spec=pltpu.PrefetchScalarGridSpec(
            num_scalar_prefetch=1,
            grid=(3,),
            in_specs=[pl.BlockSpec((1, rows, width), lambda k, c: (k, 0, 0))] * SWAPS + [HBM_REF, HBM_REF],
            out_specs=[pl.BlockSpec((1, 2, width, width), lambda k, c: (k + 3, 0, 0, 0)), pl.BlockSpec(memory_space=pltpu.VMEM)],
            scratch_shapes=[pltpu.SemaphoreType.DMA((SWAPS,))],
        ),
        out_shape=[jax.ShapeDtypeStruct(store.shape, BF16), jax.ShapeDtypeStruct((1, width, width), F32)],
        input_output_aliases={SWAPS + 1: 0},
        compiler_params=params(),
        cost_estimate=cost(),
        name="full_store",
    )(core, *received, store, env)


def near_terms(core, site, own, other, in_env, store, parts, after, first=0, states=None):
    states, width = states or own.shape[0], own.shape[-1]
    rows = width // parts

    def kernel(core_ref, a_ref, b_ref, ta_ref, tb_ref, *refs):
        a, b = (a_ref[0, 0], b_ref[0, 0]) if in_env else (a_ref[0], b_ref[0])
        total = sandwich(a, ta_ref[0, 0], ta_ref[0, 1]) + sandwich(b, tb_ref[0, 0], tb_ref[0, 1])
        for p in range(parts):
            refs[len(after) + p][0] = total[p * rows : (p + 1) * rows]

    def slot(k):
        return lambda n, c: ((3 * c[0] if site == 0 else 3 - 3 * c[0]) + k, 0, 0, 0)

    row = pl.BlockSpec((1, width, width), lambda n, c: (n, 0, 0))
    sources = [row, row]
    if in_env:
        block = (1, 1, width, width)
        sources = [pl.BlockSpec(block, lambda n, c: (n + first, c[0], 0, 0)), pl.BlockSpec(block, lambda n, c: (n + first, 1 - c[0], 0, 0))]
    pair = (1, 2, width, width)
    return pl.pallas_call(
        kernel,
        grid_spec=pltpu.PrefetchScalarGridSpec(
            num_scalar_prefetch=1,
            grid=(states,),
            in_specs=sources + [pl.BlockSpec(pair, slot(0)), pl.BlockSpec(pair, slot(1))] + [HBM_REF] * len(after),
            out_specs=[pl.BlockSpec((1, rows, width), lambda n, c: (n, 0, 0))] * parts,
        ),
        out_shape=[jax.ShapeDtypeStruct((states, rows, width), F32)] * parts,
        compiler_params=params(),
        cost_estimate=cost(),
        name=f"near_terms_{site}",
    )(core, own, other, store, store, *after)


def far_terms(core, site, partial, first, halo, store, parts, weight, after):
    states, width = halo.shape[0], halo.shape[-1]
    rows = width // parts

    def kernel(core_ref, p_ref, h_ref, t_ref, *refs):
        total = p_ref[0] + sandwich(h_ref[0], t_ref[0, 0], t_ref[0, 1])
        for p in range(parts):
            refs[len(after) + p][0] = total[p * rows : (p + 1) * rows]

    return pl.pallas_call(
        kernel,
        grid_spec=pltpu.PrefetchScalarGridSpec(
            num_scalar_prefetch=1,
            grid=(states,),
            in_specs=[
                pl.BlockSpec((1, width, width), lambda n, c: (n + first, 0, 0)),
                pl.BlockSpec((1, width, width), lambda n, c: (n, 0, 0)),
                pl.BlockSpec((1, 2, width, width), lambda n, c: ((3 * c[0] if site == 0 else 3 - 3 * c[0]) + 2, 0, 0, 0)),
            ]
            + [HBM_REF] * len(after),
            out_specs=[pl.BlockSpec((1, rows, width), lambda n, c: (n, 0, 0))] * parts,
        ),
        out_shape=[jax.ShapeDtypeStruct((states, rows, width), F32)] * parts,
        compiler_params=params(),
        cost_estimate=cost(weight),
        name=f"far_terms_{site}",
    )(core, partial, halo, store, *after)


def far_pair(core, partial, done, halo, store, weight):
    width = halo.shape[-1]

    def kernel(core_ref, p_ref, d_ref, h_ref, t_ref, o_ref):
        o_ref[0] = d_ref[0]
        o_ref[1] = p_ref[0] + sandwich(h_ref[0], t_ref[0, 0], t_ref[0, 1])

    row = pl.BlockSpec((1, width, width), lambda n, c: (0, 0, 0))
    return pl.pallas_call(
        kernel,
        grid_spec=pltpu.PrefetchScalarGridSpec(
            num_scalar_prefetch=1,
            grid=(1,),
            in_specs=[
                pl.BlockSpec((1, width, width), lambda n, c: (1, 0, 0)),
                row,
                row,
                pl.BlockSpec((1, 2, width, width), lambda n, c: (3 * c[0] + 2, 0, 0, 0)),
            ],
            out_specs=pl.BlockSpec((2, width, width), lambda n, c: (0, 0, 0)),
        ),
        out_shape=jax.ShapeDtypeStruct((2, width, width), F32),
        compiler_params=params(),
        cost_estimate=cost(weight),
        name="far_pair",
    )(core, partial, done, halo, store)


def write_rows(core, out, shape, moves, name):
    width = shape[-1]
    sources = [block for c in range(2) for blocks, _, _ in moves[c] for block in blocks]
    count = len(sources)
    old = [] if out is None else [out]

    def kernel(core_ref, *refs):
        o_ref, sems = refs[count + len(old)], refs[-1]
        if not old:
            refs[count + 1][...] = jnp.zeros((8, 128), F32)
        at = 0
        plans = []
        for c in range(2):
            plan = []
            for blocks, state, sector in moves[c]:
                rows = width // len(blocks)
                for p in range(len(blocks)):
                    plan += [(at, n, state + n, sector, p * rows, rows) for n in range(blocks[p].shape[0])]
                    at += 1
            plans.append(plan)
        for c in range(2):

            @pl.when(core_ref[0] == c)
            def _():
                copies = [
                    pltpu.make_async_copy(refs[i].at[n], o_ref.at[state, sector, pl.ds(begin, rows)], sems.at[m])
                    for m, (i, n, state, sector, begin, rows) in enumerate(plans[c])
                ]
                for copy in copies:
                    copy.start()
                for copy in copies:
                    copy.wait()

    outs = [jax.ShapeDtypeStruct(shape, F32)]
    if not old:
        outs.append(jax.ShapeDtypeStruct((8, 128), F32))
    return pl.pallas_call(
        kernel,
        grid_spec=pltpu.PrefetchScalarGridSpec(
            num_scalar_prefetch=1,
            grid=(1,),
            in_specs=[pl.BlockSpec(memory_space=pltpu.VMEM)] * count + [HBM_REF] * len(old),
            out_specs=[HBM_REF, pl.BlockSpec(memory_space=pltpu.VMEM)][: len(outs)],
            scratch_shapes=[pltpu.SemaphoreType.DMA((16,))],
        ),
        out_shape=outs,
        input_output_aliases={count + 1: 0} if old else {},
        compiler_params=params(),
        cost_estimate=cost(),
        name=name,
    )(core, *sources, *old)


RING = 4


def sooner(j):
    return (lax.rem(j, RING) == 0) * 1 if isinstance(j, jax.Array) else int(j % RING == 0)


def sooner_term(core, halo, store, after):
    width = halo.shape[-1]

    def kernel(core_ref, h_ref, t_ref, after_ref, o_ref):
        @pl.when(core_ref[0] == 1)
        def _():
            slot = 6 - 4 * sooner(lax.axis_index("blk"))
            o_ref[...] = sandwich(h_ref[0], t_ref[slot, 0], t_ref[slot, 1])

    return pl.pallas_call(
        kernel,
        grid_spec=pltpu.PrefetchScalarGridSpec(
            num_scalar_prefetch=1,
            grid=(1,),
            in_specs=[
                pl.BlockSpec((1, width, width), lambda n, c: (0, 0, 0)),
                pl.BlockSpec(memory_space=pltpu.VMEM),
                HBM_REF,
            ],
            out_specs=pl.BlockSpec((width, width), lambda n, c: (0, 0)),
        ),
        out_shape=jax.ShapeDtypeStruct((width, width), F32),
        compiler_params=params(),
        cost_estimate=cost(),
        name="sooner_term",
    )(core, halo, store, after)


def last_rows(core, out, moved, partial, near, sooner_far, halo, store):
    width = halo.shape[-1]
    rows = width // HALVES
    first = out.shape[0] - halo.shape[0]
    early = moved[0].shape[1]

    def kernel(core_ref, *refs):
        blocks, (partial_ref, near_ref, s_ref, h_ref, t_ref, _, o_ref, buf, sems, early_sems) = refs[: len(moved)], refs[len(moved) :]
        sector = sooner(lax.axis_index("blk"))

        def near_sum(chosen, span):
            return jnp.where(chosen == 0, partial_ref[0, span], near_ref[0, span])

        @pl.when(core_ref[0] == 1)
        def _():
            copies = []
            for p, block in enumerate(blocks):
                for n in range(first):
                    copies.append(pltpu.make_async_copy(block.at[n], o_ref.at[n, 0, pl.ds(p * early, early)], early_sems.at[p, n]))
                    copies[-1].start()
            slot = 2 + 4 * sector
            high, low = t_ref[slot, 0], t_ref[slot, 1]
            inner_high, inner_low = inner_halves(h_ref[0], high, low)
            buf[0] = s_ref[...] + near_sum(sector, slice(0, width))
            copies.append(pltpu.make_async_copy(buf.at[0], o_ref.at[first, sector], sems.at[HALVES]))
            copies[-1].start()
            for h in range(HALVES):
                span = slice(h * rows, (h + 1) * rows)
                buf[1, span] = near_sum(1 - sector, span) + outer(high[span], low[span], inner_high, inner_low)
                copies.append(pltpu.make_async_copy(buf.at[1, span], o_ref.at[first, 1 - sector, span], sems.at[h]))
                copies[-1].start()
            for copy in copies:
                copy.wait()

    whole = pl.BlockSpec(memory_space=pltpu.VMEM)
    count = len(moved) + 4
    return pl.pallas_call(
        kernel,
        grid_spec=pltpu.PrefetchScalarGridSpec(
            num_scalar_prefetch=1,
            grid=(1,),
            in_specs=[whole] * count + [whole, HBM_REF],
            out_specs=HBM_REF,
            scratch_shapes=[
                pltpu.VMEM((2, width, width), F32),
                pltpu.SemaphoreType.DMA((HALVES + 1,)),
                pltpu.SemaphoreType.DMA((len(moved), first)),
            ],
        ),
        out_shape=jax.ShapeDtypeStruct(out.shape, F32),
        input_output_aliases={count + 2: 0},
        compiler_params=params(),
        cost_estimate=cost(),
        name="last_rows",
    )(core, *moved, partial, near, sooner_far, halo, store, out)


def shards(chips, env_in, site_tensor, pair_live, coef_index, mpo_coef):
    axes = ("site", "blk")
    core = jnp.reshape(lax.axis_index("site"), (1,)).astype(jnp.int32)
    swap = [(s * chips + j, (1 - s) * chips + j) for s in range(2) for j in range(chips)]
    meet = [(chips + j, j + 1) for j in range(chips - 1)] + [(j + 1, chips + j) for j in range(chips - 1)]

    from_left = {j: (chips + j - 1, chips + j) for j in range(1, chips)}
    from_right = {j: (j + 1, chips + j) for j in range(chips - 1)}
    sides = from_left, from_right
    soon = [sides[sooner(j)][j] for j in range(chips) if j in sides[sooner(j)]]
    later = [sides[1 - sooner(j)][j] for j in range(chips) if j in sides[1 - sooner(j)]]

    def send(value, pairs):
        return lax.ppermute(value, axes, pairs)

    scalars = (pair_live, coef_index, mpo_coef)
    pinned = pltpu.with_memory_space_constraint(env_in, pltpu.HBM)
    edge_0 = edge(core, pinned)
    halo_0 = send(edge_0, meet)
    leaving = outgoing(core, scalars, site_tensor, edge_0)
    received = [send(block, swap) for block in leaving]
    store, edge_1 = own_store(core, scalars, site_tensor, pinned, leaving[0])
    halo_1 = send(edge_1, meet)
    store, edge_2 = full_store(core, store, received, pinned)
    halo_2 = send(edge_2, meet)

    (near_01,) = near_terms(core, 0, env_in, env_in, True, store, 1, [], 0, CUTS)
    (first_0,) = far_terms(core, 0, near_01, 0, halo_0, store, 1, 16, [])
    first_a = far_pair(core, near_01, first_0, halo_1, store, 0)
    second_halo_a, crossed_a = send(first_a, meet), send(first_a, swap)
    (near_2,) = near_terms(core, 0, env_in, env_in, True, store, 1, [first_a], CUTS, 3 - CUTS)
    (first_b,) = far_terms(core, 0, near_2, 0, halo_2, store, 1, 0, [first_a])
    halo_soon, halo_later, crossed_b = send(first_b, soon), send(first_b, later), send(first_b, swap)

    (near_a,) = near_terms(core, 1, first_a, crossed_a, False, store, 1, [])
    sums = near_terms(core, 1, first_b, crossed_b, False, store, PARTS, [near_a])
    partials = [send(block, swap) for block in sums]
    second_a = far_terms(core, 1, near_a, 0, second_halo_a, store, 2, 0, sums[:1])
    moved_a = [send(block, swap) for block in second_a]
    early = [([first_a], 0, 0), ([crossed_a], 0, 1), ([first_b], CUTS, 0), ([crossed_b], CUTS, 1)], [(second_a, 0, 1)]
    out, mark = write_rows(core, None, env_in.shape, early, "early_rows")
    sooner_far = sooner_term(core, halo_soon, store, mark)
    out = last_rows(core, out, moved_a, *partials, *sums, sooner_far, halo_later, store)
    return out[None]


def solution(mesh):
    return jax.shard_map(
        functools.partial(shards, mesh.shape["blk"]),
        mesh=mesh,
        in_specs=(
            P(None, "blk", None, None),
            P("site", "blk", None, None, None),
            P("site", "blk", None),
            P("site", "blk", None),
            P("site", None),
        ),
        out_specs=P("site", None, "blk", None, None),
        check_vma=False,
    )
```

```python
import functools

import jax
import jax.numpy as jnp
from jax import lax
from jax.experimental import pallas as pl
from jax.experimental.pallas import tpu as pltpu
from jax.sharding import PartitionSpec as P

F32 = jnp.float32
BF16 = jnp.bfloat16
LIMIT = 28 << 20

STORE = 7
CUTS = 2
SWAPS = 4
PARTS = 1
HALVES = 2


def split(x):
    high = x.astype(BF16)
    return high, (x - high.astype(F32)).astype(BF16)


def dot_nn(a, b):
    return jnp.dot(a, b, preferred_element_type=F32)


def dot_nt(a, b):
    return lax.dot_general(a, b, (((1,), (1,)), ((), ())), preferred_element_type=F32)


def inner_halves(block, high, low):
    block_high, block_low = split(block)
    return split(dot_nt(block_high, high) + dot_nt(block_high, low) + dot_nt(block_low, high))


def outer(high, low, inner_high, inner_low):
    return dot_nn(high, inner_high) + dot_nn(low, inner_high) + dot_nn(high, inner_low)


def sandwich(block, high, low):
    return outer(high, low, *inner_halves(block, high, low))


def cost(weight=0.0):
    return pl.CostEstimate(flops=int(weight * 1.15e9), bytes_accessed=1024, transcendentals=0)


def params():
    return pltpu.CompilerParams(vmem_limit_bytes=LIMIT)


def root(live_ref, index_ref, coef_ref, sector, slot, width):
    weight = live_ref[0, sector, slot].astype(F32) * coef_ref[0, index_ref[0, sector, slot]]
    return jnp.sqrt(jnp.full((1, width), weight, F32))


def slot_at(k, c):
    return jnp.where(k == 0, 1, jnp.where(k == 1, 2 - 2 * c, 2 * c))


SCALARS = [pl.BlockSpec(memory_space=pltpu.SMEM)] * 3
HBM_REF = pl.BlockSpec(memory_space=pl.ANY)


def edge(core, env):
    width = env.shape[-1]
    parts = 2
    rows = width // parts

    def kernel(core_ref, e_ref, o_ref, sems):
        copies = []
        for n in range(1):
            for p in range(parts):
                span = pl.ds(p * rows, rows)
                copies.append(pltpu.make_async_copy(e_ref.at[n, core_ref[0], span], o_ref.at[n, span], sems.at[n * parts + p]))
        for copy in copies:
            copy.start()
        for copy in copies:
            copy.wait()

    return pl.pallas_call(
        kernel,
        grid_spec=pltpu.PrefetchScalarGridSpec(
            num_scalar_prefetch=1,
            grid=(1,),
            in_specs=[HBM_REF],
            out_specs=pl.BlockSpec(memory_space=pltpu.VMEM),
            scratch_shapes=[pltpu.SemaphoreType.DMA((parts,))],
        ),
        out_shape=jax.ShapeDtypeStruct((1, width, width), F32),
        compiler_params=params(),
        cost_estimate=cost(),
        name="edge",
    )(core, env)


def outgoing(core, scalars, tensors, after):
    width = tensors.shape[-1]
    rows = width // SWAPS

    def kernel(core_ref, live_ref, index_ref, coef_ref, t_ref, after_ref, *o_refs):
        other = 1 - core_ref[0]
        for k in range(3):
            slot = slot_at(k, other)
            scaled = t_ref[0, 0, slot] * root(live_ref, index_ref, coef_ref, other, slot, width)
            for p, o_ref in enumerate(o_refs):
                o_ref[k] = scaled[p * rows : (p + 1) * rows]

    return pl.pallas_call(
        kernel,
        grid_spec=pltpu.PrefetchScalarGridSpec(
            num_scalar_prefetch=1,
            grid=(1,),
            in_specs=SCALARS + [pl.BlockSpec((1, 1, 3, width, width), lambda k, c: (0, 1 - c[0], 0, 0, 0)), HBM_REF],
            out_specs=[pl.BlockSpec((3, rows, width), lambda k, c: (0, 0, 0))] * SWAPS,
        ),
        out_shape=[jax.ShapeDtypeStruct((3, rows, width), F32)] * SWAPS,
        compiler_params=params(),
        cost_estimate=cost(),
        name="outgoing",
    )(core, *scalars, tensors, after)


def own_store(core, scalars, tensors, env, after):
    width = tensors.shape[-1]

    def kernel(core_ref, live_ref, index_ref, coef_ref, t_ref, e_ref, after_ref, o_ref, edge_ref, sems):
        c = core_ref[0]
        k = pl.program_id(0)
        slot = jnp.where(k < 3, slot_at(k, c), 0)
        parts = 4
        copies = []
        for p in range(parts):
            span = pl.ds(p * (width // parts), width // parts)
            copies.append(pltpu.make_async_copy(e_ref.at[1, c, span], edge_ref.at[0, span], sems.at[p]))

        @pl.when(k == 0)
        def _():
            for copy in copies:
                copy.start()

        high, low = split((t_ref[0, 0, 0] * root(live_ref, index_ref, coef_ref, jnp.where(k < 3, c, 1 - c), slot, width)).T)
        o_ref[0, 0] = high
        o_ref[0, 1] = low

        @pl.when(k == 3)
        def _():
            for copy in copies:
                copy.wait()

    return pl.pallas_call(
        kernel,
        grid_spec=pltpu.PrefetchScalarGridSpec(
            num_scalar_prefetch=1,
            grid=(4,),
            in_specs=SCALARS + [pl.BlockSpec((1, 1, 1, width, width), lambda k, c: (0, jnp.where(k < 3, c[0], 1 - c[0]), jnp.where(k < 3, slot_at(k, c[0]), 0), 0, 0)), HBM_REF, HBM_REF],
            out_specs=[pl.BlockSpec((1, 2, width, width), lambda k, c: (jnp.where(k < 3, k, 6), 0, 0, 0)), pl.BlockSpec(memory_space=pltpu.VMEM)],
            scratch_shapes=[pltpu.SemaphoreType.DMA((4,))],
        ),
        out_shape=[jax.ShapeDtypeStruct((STORE, 2, width, width), BF16), jax.ShapeDtypeStruct((1, width, width), F32)],
        compiler_params=params(),
        cost_estimate=cost(),
        name="own_store",
    )(core, *scalars, tensors, env, after)


def full_store(core, store, received, env):
    width = store.shape[-1]
    rows = width // SWAPS

    def kernel(core_ref, *refs):
        blocks, (_, e_ref, o_ref, edge_ref, sems) = refs[:SWAPS], refs[SWAPS:]
        k = pl.program_id(0)
        copies = []
        for p in range(SWAPS):
            span = pl.ds(p * rows, rows)
            copies.append(pltpu.make_async_copy(e_ref.at[2, core_ref[0], span], edge_ref.at[0, span], sems.at[p]))

        @pl.when(k == 0)
        def _():
            for copy in copies:
                copy.start()

        high, low = split(jnp.concatenate([block[0] for block in blocks], 0).T)
        o_ref[0, 0] = high
        o_ref[0, 1] = low

        @pl.when(k == 2)
        def _():
            for copy in copies:
                copy.wait()

    return pl.pallas_call(
        kernel,
        grid_spec=pltpu.PrefetchScalarGridSpec(
            num_scalar_prefetch=1,
            grid=(3,),
            in_specs=[pl.BlockSpec((1, rows, width), lambda k, c: (k, 0, 0))] * SWAPS + [HBM_REF, HBM_REF],
            out_specs=[pl.BlockSpec((1, 2, width, width), lambda k, c: (k + 3, 0, 0, 0)), pl.BlockSpec(memory_space=pltpu.VMEM)],
            scratch_shapes=[pltpu.SemaphoreType.DMA((SWAPS,))],
        ),
        out_shape=[jax.ShapeDtypeStruct(store.shape, BF16), jax.ShapeDtypeStruct((1, width, width), F32)],
        input_output_aliases={SWAPS + 1: 0},
        compiler_params=params(),
        cost_estimate=cost(),
        name="full_store",
    )(core, *received, store, env)


def near_terms(core, site, own, other, in_env, store, parts, after, first=0, states=None):
    states, width = states or own.shape[0], own.shape[-1]
    rows = width // parts

    def kernel(core_ref, a_ref, b_ref, ta_ref, tb_ref, *refs):
        a, b = (a_ref[0, 0], b_ref[0, 0]) if in_env else (a_ref[0], b_ref[0])
        total = sandwich(a, ta_ref[0, 0], ta_ref[0, 1]) + sandwich(b, tb_ref[0, 0], tb_ref[0, 1])
        for p in range(parts):
            refs[len(after) + p][0] = total[p * rows : (p + 1) * rows]

    def slot(k):
        return lambda n, c: ((3 * c[0] if site == 0 else 3 - 3 * c[0]) + k, 0, 0, 0)

    row = pl.BlockSpec((1, width, width), lambda n, c: (n, 0, 0))
    sources = [row, row]
    if in_env:
        block = (1, 1, width, width)
        sources = [pl.BlockSpec(block, lambda n, c: (n + first, c[0], 0, 0)), pl.BlockSpec(block, lambda n, c: (n + first, 1 - c[0], 0, 0))]
    pair = (1, 2, width, width)
    return pl.pallas_call(
        kernel,
        grid_spec=pltpu.PrefetchScalarGridSpec(
            num_scalar_prefetch=1,
            grid=(states,),
            in_specs=sources + [pl.BlockSpec(pair, slot(0)), pl.BlockSpec(pair, slot(1))] + [HBM_REF] * len(after),
            out_specs=[pl.BlockSpec((1, rows, width), lambda n, c: (n, 0, 0))] * parts,
        ),
        out_shape=[jax.ShapeDtypeStruct((states, rows, width), F32)] * parts,
        compiler_params=params(),
        cost_estimate=cost(),
        name=f"near_terms_{site}",
    )(core, own, other, store, store, *after)


def far_terms(core, site, partial, first, halo, store, parts, weight, after):
    states, width = halo.shape[0], halo.shape[-1]
    rows = width // parts

    def kernel(core_ref, p_ref, h_ref, t_ref, *refs):
        total = p_ref[0] + sandwich(h_ref[0], t_ref[0, 0], t_ref[0, 1])
        for p in range(parts):
            refs[len(after) + p][0] = total[p * rows : (p + 1) * rows]

    return pl.pallas_call(
        kernel,
        grid_spec=pltpu.PrefetchScalarGridSpec(
            num_scalar_prefetch=1,
            grid=(states,),
            in_specs=[
                pl.BlockSpec((1, width, width), lambda n, c: (n + first, 0, 0)),
                pl.BlockSpec((1, width, width), lambda n, c: (n, 0, 0)),
                pl.BlockSpec((1, 2, width, width), lambda n, c: ((3 * c[0] if site == 0 else 3 - 3 * c[0]) + 2, 0, 0, 0)),
            ]
            + [HBM_REF] * len(after),
            out_specs=[pl.BlockSpec((1, rows, width), lambda n, c: (n, 0, 0))] * parts,
        ),
        out_shape=[jax.ShapeDtypeStruct((states, rows, width), F32)] * parts,
        compiler_params=params(),
        cost_estimate=cost(weight),
        name=f"far_terms_{site}",
    )(core, partial, halo, store, *after)


def far_pair(core, partial, done, halo, store, weight):
    width = halo.shape[-1]

    def kernel(core_ref, p_ref, d_ref, h_ref, t_ref, o_ref):
        o_ref[0] = d_ref[0]
        o_ref[1] = p_ref[0] + sandwich(h_ref[0], t_ref[0, 0], t_ref[0, 1])

    row = pl.BlockSpec((1, width, width), lambda n, c: (0, 0, 0))
    return pl.pallas_call(
        kernel,
        grid_spec=pltpu.PrefetchScalarGridSpec(
            num_scalar_prefetch=1,
            grid=(1,),
            in_specs=[
                pl.BlockSpec((1, width, width), lambda n, c: (1, 0, 0)),
                row,
                row,
                pl.BlockSpec((1, 2, width, width), lambda n, c: (3 * c[0] + 2, 0, 0, 0)),
            ],
            out_specs=pl.BlockSpec((2, width, width), lambda n, c: (0, 0, 0)),
        ),
        out_shape=jax.ShapeDtypeStruct((2, width, width), F32),
        compiler_params=params(),
        cost_estimate=cost(weight),
        name="far_pair",
    )(core, partial, done, halo, store)


def write_rows(core, out, shape, moves, name):
    width = shape[-1]
    sources = [block for c in range(2) for blocks, _, _ in moves[c] for block in blocks]
    count = len(sources)
    old = [] if out is None else [out]

    def kernel(core_ref, *refs):
        o_ref, sems = refs[count + len(old)], refs[-1]
        if not old:
            refs[count + 1][...] = jnp.zeros((8, 128), F32)
        at = 0
        plans = []
        for c in range(2):
            plan = []
            for blocks, state, sector in moves[c]:
                rows = width // len(blocks)
                for p in range(len(blocks)):
                    plan += [(at, n, state + n, sector, p * rows, rows) for n in range(blocks[p].shape[0])]
                    at += 1
            plans.append(plan)
        for c in range(2):

            @pl.when(core_ref[0] == c)
            def _():
                copies = [
                    pltpu.make_async_copy(refs[i].at[n], o_ref.at[state, sector, pl.ds(begin, rows)], sems.at[m])
                    for m, (i, n, state, sector, begin, rows) in enumerate(plans[c])
                ]
                for copy in copies:
                    copy.start()
                for copy in copies:
                    copy.wait()

    outs = [jax.ShapeDtypeStruct(shape, F32)]
    if not old:
        outs.append(jax.ShapeDtypeStruct((8, 128), F32))
    return pl.pallas_call(
        kernel,
        grid_spec=pltpu.PrefetchScalarGridSpec(
            num_scalar_prefetch=1,
            grid=(1,),
            in_specs=[pl.BlockSpec(memory_space=pltpu.VMEM)] * count + [HBM_REF] * len(old),
            out_specs=[HBM_REF, pl.BlockSpec(memory_space=pltpu.VMEM)][: len(outs)],
            scratch_shapes=[pltpu.SemaphoreType.DMA((16,))],
        ),
        out_shape=outs,
        input_output_aliases={count + 1: 0} if old else {},
        compiler_params=params(),
        cost_estimate=cost(),
        name=name,
    )(core, *sources, *old)


RING = 4


def sooner(j):
    return (lax.rem(j, RING) == 0) * 1 if isinstance(j, jax.Array) else int(j % RING == 0)


def sooner_term(core, halo, store, after):
    width = halo.shape[-1]

    def kernel(core_ref, h_ref, t_ref, after_ref, o_ref):
        @pl.when(core_ref[0] == 1)
        def _():
            slot = 6 - 4 * sooner(lax.axis_index("blk"))
            o_ref[...] = sandwich(h_ref[0], t_ref[slot, 0], t_ref[slot, 1])

    return pl.pallas_call(
        kernel,
        grid_spec=pltpu.PrefetchScalarGridSpec(
            num_scalar_prefetch=1,
            grid=(1,),
            in_specs=[
                pl.BlockSpec((1, width, width), lambda n, c: (0, 0, 0)),
                pl.BlockSpec(memory_space=pltpu.VMEM),
                HBM_REF,
            ],
            out_specs=pl.BlockSpec((width, width), lambda n, c: (0, 0)),
        ),
        out_shape=jax.ShapeDtypeStruct((width, width), F32),
        compiler_params=params(),
        cost_estimate=cost(),
        name="sooner_term",
    )(core, halo, store, after)


def last_rows(core, out, moved, partial, near, sooner_far, halo, store):
    width = halo.shape[-1]
    rows = width // HALVES
    first = out.shape[0] - halo.shape[0]
    early = moved[0].shape[1]

    def kernel(core_ref, *refs):
        blocks, (partial_ref, near_ref, s_ref, h_ref, t_ref, _, o_ref, buf, sems, early_sems) = refs[: len(moved)], refs[len(moved) :]
        sector = sooner(lax.axis_index("blk"))

        def near_sum(chosen, span):
            return jnp.where(chosen == 0, partial_ref[0, span], near_ref[0, span])

        @pl.when(core_ref[0] == 1)
        def _():
            copies = []
            for p, block in enumerate(blocks):
                for n in range(first):
                    copies.append(pltpu.make_async_copy(block.at[n], o_ref.at[n, 0, pl.ds(p * early, early)], early_sems.at[p, n]))
                    copies[-1].start()
            buf[0] = s_ref[...] + near_sum(sector, slice(0, width))
            copies.append(pltpu.make_async_copy(buf.at[0], o_ref.at[first, sector], sems.at[HALVES]))
            copies[-1].start()
            slot = 2 + 4 * sector
            high, low = t_ref[slot, 0], t_ref[slot, 1]
            inner_high, inner_low = inner_halves(h_ref[0], high, low)
            for h in range(HALVES):
                span = slice(h * rows, (h + 1) * rows)
                buf[1, span] = near_sum(1 - sector, span) + outer(high[span], low[span], inner_high, inner_low)
                copies.append(pltpu.make_async_copy(buf.at[1, span], o_ref.at[first, 1 - sector, span], sems.at[h]))
                copies[-1].start()
            for copy in copies:
                copy.wait()

    whole = pl.BlockSpec(memory_space=pltpu.VMEM)
    count = len(moved) + 4
    return pl.pallas_call(
        kernel,
        grid_spec=pltpu.PrefetchScalarGridSpec(
            num_scalar_prefetch=1,
            grid=(1,),
            in_specs=[whole] * count + [whole, HBM_REF],
            out_specs=HBM_REF,
            scratch_shapes=[
                pltpu.VMEM((2, width, width), F32),
                pltpu.SemaphoreType.DMA((HALVES + 1,)),
                pltpu.SemaphoreType.DMA((len(moved), first)),
            ],
        ),
        out_shape=jax.ShapeDtypeStruct(out.shape, F32),
        input_output_aliases={count + 2: 0},
        compiler_params=params(),
        cost_estimate=cost(),
        name="last_rows",
    )(core, *moved, partial, near, sooner_far, halo, store, out)


def shards(chips, env_in, site_tensor, pair_live, coef_index, mpo_coef):
    axes = ("site", "blk")
    core = jnp.reshape(lax.axis_index("site"), (1,)).astype(jnp.int32)
    swap = [(s * chips + j, (1 - s) * chips + j) for s in range(2) for j in range(chips)]
    meet = [(chips + j, j + 1) for j in range(chips - 1)] + [(j + 1, chips + j) for j in range(chips - 1)]

    from_left = {j: (chips + j - 1, chips + j) for j in range(1, chips)}
    from_right = {j: (j + 1, chips + j) for j in range(chips - 1)}
    sides = from_left, from_right
    soon = [sides[sooner(j)][j] for j in range(chips) if j in sides[sooner(j)]]
    later = [sides[1 - sooner(j)][j] for j in range(chips) if j in sides[1 - sooner(j)]]

    def send(value, pairs):
        return lax.ppermute(value, axes, pairs)

    scalars = (pair_live, coef_index, mpo_coef)
    pinned = pltpu.with_memory_space_constraint(env_in, pltpu.HBM)
    edge_0 = edge(core, pinned)
    halo_0 = send(edge_0, meet)
    leaving = outgoing(core, scalars, site_tensor, edge_0)
    received = [send(block, swap) for block in leaving]
    store, edge_1 = own_store(core, scalars, site_tensor, pinned, leaving[0])
    halo_1 = send(edge_1, meet)
    store, edge_2 = full_store(core, store, received, pinned)
    halo_2 = send(edge_2, meet)

    (near_01,) = near_terms(core, 0, env_in, env_in, True, store, 1, [], 0, CUTS)
    (first_0,) = far_terms(core, 0, near_01, 0, halo_0, store, 1, 16, [])
    first_a = far_pair(core, near_01, first_0, halo_1, store, 0)
    second_halo_a, crossed_a = send(first_a, meet), send(first_a, swap)
    (near_2,) = near_terms(core, 0, env_in, env_in, True, store, 1, [first_a], CUTS, 3 - CUTS)
    (first_b,) = far_terms(core, 0, near_2, 0, halo_2, store, 1, 0, [first_a])
    halo_soon, halo_later, crossed_b = send(first_b, soon), send(first_b, later), send(first_b, swap)

    (near_a,) = near_terms(core, 1, first_a, crossed_a, False, store, 1, [])
    sums = near_terms(core, 1, first_b, crossed_b, False, store, PARTS, [near_a])
    partials = [send(block, swap) for block in sums]
    second_a = far_terms(core, 1, near_a, 0, second_halo_a, store, 2, 0, sums[:1])
    moved_a = [send(block, swap) for block in second_a]
    early = [([first_a], 0, 0), ([crossed_a], 0, 1), ([first_b], CUTS, 0), ([crossed_b], CUTS, 1)], [(second_a, 0, 1)]
    out, mark = write_rows(core, None, env_in.shape, early, "early_rows")
    sooner_far = sooner_term(core, halo_soon, store, mark)
    out = last_rows(core, out, moved_a, *partials, *sums, sooner_far, halo_later, store)
    return out[None]


def solution(mesh):
    return jax.shard_map(
        functools.partial(shards, mesh.shape["blk"]),
        mesh=mesh,
        in_specs=(
            P(None, "blk", None, None),
            P("site", "blk", None, None, None),
            P("site", "blk", None),
            P("site", "blk", None),
            P("site", None),
        ),
        out_specs=P("site", None, "blk", None, None),
        check_vma=False,
    )
```
